128 devices in a mesh: ctx: 32 (over x, y, core), head: 4 (over z).
Axes of the slice: x: 4, y: 4, z: 4, core: 2. Of those that a mesh axis runs over, the one named last changes fastest.
Arguments:
- queries: bfloat16 [32, 8, 64, 3072], P('ctx', None, None, 'head'), may hold values from -160 to 160
- keys: bfloat16 [32, 8, 64, 3072], P('ctx', None, None, 'head'), may hold values from -7 to 7
- values: bfloat16 [32, 8, 64, 3072], P('ctx', None, None, 'head'), may hold values from -6 to 6
- out_grad: bfloat16 [32, 8, 64, 3072], P('ctx', None, None, 'head'), may hold values from -6 to 6
- window_mask: int32 [32, 8, 27], P('ctx'), may hold values 0 or 1
Outputs:
- query_gradient: bfloat16 [32, 8, 64, 3072], P('ctx', None, None, 'head')
- key_gradient: bfloat16 [32, 8, 64, 3072], P('ctx', None, None, 'head')
- value_gradient: bfloat16 [32, 8, 64, 3072], P('ctx', None, None, 'head')
The draws below stay inside these ranges and needn't reach their ends.
All inputs are finite; a program needn't handle non-finite values. No bound on the sum of `window_mask` on one device may be relied on, other than what follows from the above.
Results may differ from the reference program's by a relative error of at most 0.015.
Values may be sent and summed in bfloat16 or wider, within the bound.
No kernel may reach another device: no remote copies, remote signals or barrier semaphores. Data moves between devices by JAX's collectives and lax.ppermute only.
A program may use at most 192 MiB of HBM per device.

```python
import jax
import jax.numpy as jnp
from jax import lax

HEADS = 24
HEAD_DIM = 128
TILE = 4
ROW_BLOCKS = 2
FRAMES = 32
HEIGHT = 8
WIDTH = 64


def shared_normal(key):
    shape = (FRAMES, HEIGHT, WIDTH, HEADS * HEAD_DIM)
    return jnp.clip(jax.random.normal(jax.random.fold_in(key, 500), shape, jnp.float32), -6.0, 6.0)


def paired_keys(key, wobble):
    base = shared_normal(key)
    noise = jnp.clip(jax.random.normal(jax.random.fold_in(key, 501), base.shape, jnp.float32), -6.0, 6.0)
    even = base[:, :, 0::2]
    odd = even * 1.01 + wobble * noise[:, :, 0::2]
    return jnp.stack([even, odd], axis=3).reshape(base.shape)


def draw_keys(key, part):
    paired = paired_keys(key, 0.05)
    key = jax.random.fold_in(key, 3)
    return jnp.clip(jax.random.normal(key, paired.shape, jnp.float32), -6.0, 6.0).astype(jnp.bfloat16)


def draw_queries(key, part):
    paired = paired_keys(key, 0.05)
    key = jax.random.fold_in(key, 4)
    second = jax.random.fold_in(key, 1)
    shape = paired.shape
    return jnp.clip(jax.random.normal(second, shape, jnp.float32), -6.0, 6.0).astype(jnp.bfloat16)


def plant(drawn, rng, smallest, largest):
    longest = drawn.shape.index(max(drawn.shape))
    spots = []
    for shift in (0, 1):
        where = [jax.random.randint(jax.random.fold_in(rng, axis), (), 0, length) for axis, length in enumerate(drawn.shape)]
        where[longest] = (where[longest] + shift) % drawn.shape[longest]
        spots.append(tuple(where))
    return drawn.at[spots[0]].set(smallest).at[spots[1]].set(largest)


def block_levels(rng, extent, shards, least, top_value):
    factor_of, own = 1.0, jax.random.fold_in(rng, 6)
    for axis_at, blocks in shards:
        heights = jnp.exp(jax.random.uniform(jax.random.fold_in(own, axis_at), (blocks,), jnp.float32, least / len(shards), top_value / len(shards)))
        factor_of = factor_of * jnp.repeat(heights, extent[axis_at] // blocks).reshape([-1 if axis == axis_at else 1 for axis in range(len(extent))])
    return factor_of


def normal_values(stream_key, shape, scale, most, shards=(), dtype=jnp.bfloat16):
    values = scale * jax.random.normal(stream_key, shape, jnp.float32)
    if shards:
        values = values * block_levels(stream_key, shape, shards, -0.22, 0.18)
    return jnp.clip(values, -most, most).astype(dtype)


def setup_inputs(seed: int = 0) -> dict:
    splits = jax.random.split(jax.random.key(seed), 6)
    queries = draw_queries(jax.random.fold_in(splits[5], 71), 0)
    keys = draw_keys(jax.random.fold_in(splits[5], 71), 0)
    values = normal_values(splits[2], (FRAMES, HEIGHT, WIDTH, HEADS * HEAD_DIM), 1.0, 6.0, ((0, 32), (3, 4)))
    out_grad = normal_values(splits[3], (FRAMES, HEIGHT, WIDTH, HEADS * HEAD_DIM), 1.0, 6.0, ((0, 32), (3, 4)))
    window_mask = plant((jax.random.randint(splits[4], (HEIGHT // TILE * (WIDTH // TILE), FRAMES // TILE, 27), 0, 3) < 2).astype(jnp.int32), jax.random.fold_in(splits[4], 1), 0, 1)
    return {"queries": queries, "keys": keys, "values": values, "out_grad": out_grad, "window_mask": window_mask}


NEG_FILL = -1.0e30


def to_tiles(tensor):
    frames, height, columns_all, channels = tensor.shape
    shaped = tensor.reshape(frames // TILE, TILE, height // TILE, TILE, columns_all // TILE, TILE, channels)
    shaped = shaped.transpose(0, 2, 4, 1, 3, 5, 6)
    return shaped.reshape(frames // TILE, height // TILE, columns_all // TILE, TILE ** 3, channels)


def from_tiles(cube_array):
    time_blocks, row_blocks, col_blocks = cube_array.shape[0], cube_array.shape[1], cube_array.shape[2]
    channels = cube_array.shape[4]
    shaped = cube_array.reshape(time_blocks, row_blocks, col_blocks, TILE, TILE, TILE, channels)
    shaped = shaped.transpose(0, 3, 1, 4, 2, 5, 6)
    return shaped.reshape(time_blocks * TILE, row_blocks * TILE, col_blocks * TILE, channels)


def window_allowed(window_mask):
    time_blocks = window_mask.shape[1]
    row_blocks = ROW_BLOCKS
    col_blocks = window_mask.shape[0] // ROW_BLOCKS
    grid_mask = window_mask.reshape(row_blocks, col_blocks, time_blocks, 27).transpose(2, 0, 1, 3)
    offset = jnp.arange(27)
    time_pos = jnp.arange(time_blocks)[:, None, None, None] + offset // 9 - 1
    row_pos = jnp.arange(row_blocks)[None, :, None, None] + offset // 3 % 3 - 1
    col_pos = jnp.arange(col_blocks)[None, None, :, None] + offset % 3 - 1
    inside = (time_pos >= 0) & (time_pos < time_blocks) & (row_pos >= 0) & (row_pos < row_blocks)
    inside = inside & (col_pos >= 0) & (col_pos < col_blocks)
    chosen = (grid_mask == 1) | (offset == 13)
    return inside & chosen


def tile_grads(query_row_matrix, key_row_matrix, value_row_matrix, gradient_row_values, allowed):
    softmax_scale_factor = HEAD_DIM ** -0.5
    mask_rows = allowed[:, None, :]
    score_matrix = jnp.einsum("wfl,wzl->wfz", query_row_matrix.astype(jnp.float32), key_row_matrix.astype(jnp.float32)) * softmax_scale_factor
    score_matrix = jnp.where(mask_rows, score_matrix, NEG_FILL)
    row_max = jnp.max(score_matrix, axis=-1, keepdims=True)
    weights = jnp.where(mask_rows, jnp.exp(score_matrix - row_max), 0.0)
    attention = weights / jnp.sum(weights, axis=-1, keepdims=True)
    attention_lower_precision = attention.astype(jnp.bfloat16)
    output_rows = jnp.einsum("uap,ups->uas", attention_lower_precision.astype(jnp.float32), value_row_matrix.astype(jnp.float32))
    row_dot = jnp.sum(gradient_row_values.astype(jnp.float32) * output_rows, axis=-1)
    probability_gradient = jnp.einsum("wfl,wzl->wfz", gradient_row_values.astype(jnp.float32), value_row_matrix.astype(jnp.float32))
    score_gradient = (attention * (probability_gradient - row_dot[:, :, None]) * softmax_scale_factor).astype(jnp.bfloat16)
    query_gradient = jnp.einsum("uap,ups->uas", score_gradient.astype(jnp.float32), key_row_matrix.astype(jnp.float32))
    key_gradient = jnp.einsum("arp,arf->apf", score_gradient.astype(jnp.float32), query_row_matrix.astype(jnp.float32))
    value_gradient = jnp.einsum("arp,arf->apf", attention_lower_precision.astype(jnp.float32), gradient_row_values.astype(jnp.float32))
    return query_gradient, key_gradient, value_gradient


def head_grads(operands, allowed):
    query_cubes, key_cubes, value_cubes, grad_cubes = operands
    time_blocks, row_blocks, col_blocks, cube_cells = query_cubes.shape[0], query_cubes.shape[1], query_cubes.shape[2], query_cubes.shape[3]
    pad_spec = ((1, 1), (1, 1), (1, 1), (0, 0), (0, 0))
    key_pad = jnp.pad(key_cubes, pad_spec)
    value_pad = jnp.pad(value_cubes, pad_spec)
    tiles_block = row_blocks * col_blocks

    def gather_window(block_slab):
        pieces = [block_slab[offset_id // 9, offset_id // 3 % 3:offset_id // 3 % 3 + row_blocks, offset_id % 3:offset_id % 3 + col_blocks] for offset_id in range(27)]
        return jnp.stack(pieces, axis=2).reshape(tiles_block, 27 * cube_cells, HEAD_DIM)

    def spread(grad_acc, contrib, frame_block):
        contrib = contrib.reshape(row_blocks, col_blocks, 27, cube_cells, HEAD_DIM)
        acc_slab = lax.dynamic_slice_in_dim(grad_acc, frame_block, 3, 1)
        for offset_id in range(27):
            row_shift = offset_id // 3 % 3
            col_shift = offset_id % 3
            acc_slab = acc_slab.at[row_shift * 3 + col_shift, offset_id // 9, row_shift:row_shift + row_blocks, col_shift:col_shift + col_blocks].add(contrib[:, :, offset_id])
        return lax.dynamic_update_slice_in_dim(grad_acc, acc_slab, frame_block, 1)

    def one_block(accums, frame_block):
        key_acc, value_acc = accums
        key_row_matrix = gather_window(lax.dynamic_slice_in_dim(key_pad, frame_block, 3, 0))
        value_row_matrix = gather_window(lax.dynamic_slice_in_dim(value_pad, frame_block, 3, 0))
        block_allowed = lax.dynamic_index_in_dim(allowed, frame_block, 0, keepdims=False).reshape(tiles_block, 27)
        rows_allowed = jnp.repeat(block_allowed, cube_cells, axis=1)
        query_row_matrix = lax.dynamic_index_in_dim(query_cubes, frame_block, 0, keepdims=False).reshape(tiles_block, cube_cells, HEAD_DIM)
        gradient_row_values = lax.dynamic_index_in_dim(grad_cubes, frame_block, 0, keepdims=False).reshape(tiles_block, cube_cells, HEAD_DIM)
        query_gradient, key_gradient, value_gradient = tile_grads(query_row_matrix, key_row_matrix, value_row_matrix, gradient_row_values, rows_allowed)
        key_acc = spread(key_acc, key_gradient, frame_block)
        value_acc = spread(value_acc, value_gradient, frame_block)
        return (key_acc, value_acc), query_gradient.astype(jnp.bfloat16).reshape(row_blocks, col_blocks, cube_cells, HEAD_DIM)

    acc_shape = (9, time_blocks + 2, row_blocks + 2, col_blocks + 2, cube_cells, HEAD_DIM)
    zero_acc = jnp.zeros(acc_shape, jnp.float32)
    (key_acc, value_acc), query_gradient = lax.scan(one_block, (zero_acc, zero_acc), jnp.arange(time_blocks).astype(jnp.int32))

    def combine(grad_acc):
        parts_low = lax.optimization_barrier(grad_acc[:, 1:-1, 1:-1, 1:-1].astype(jnp.bfloat16))
        return jnp.sum(parts_low.astype(jnp.float32), axis=0).astype(jnp.bfloat16)

    return query_gradient, combine(key_acc), combine(value_acc)


def reference(queries, keys, values, out_grad, window_mask):
    allowed = window_allowed(window_mask)

    def split_heads(tensor):
        cube_array = to_tiles(tensor)
        cube_array = cube_array.reshape(cube_array.shape[:4] + (HEADS, HEAD_DIM))
        return jnp.moveaxis(cube_array, 4, 0)

    def per_head(operands):
        return head_grads(operands, allowed)

    grads = lax.map(per_head, (split_heads(queries), split_heads(keys), split_heads(values), split_heads(out_grad)))

    def join_heads(stacked):
        moved = jnp.moveaxis(stacked, 0, 4)
        return from_tiles(moved.reshape(moved.shape[:4] + (HEADS * HEAD_DIM,)))

    return join_heads(grads[0]), join_heads(grads[1]), join_heads(grads[2])
```

```python
import functools

import jax
import jax.numpy as jnp
from jax import lax
from jax.experimental import pallas as pl
from jax.experimental.pallas import tpu as pltpu
from jax.sharding import PartitionSpec as P

HEAD_DIM = 128
TILE = 4
ROW_BLOCKS = 2
NEG_FILL = -1e30
SCALE = HEAD_DIM ** (-0.5)
LOG2E = 1.4426950408889634
HEADS_LOCAL = 3
BLOCK = ROW_BLOCKS * TILE**3
STEPS = (-1, 0, 1)

XS, HALVES, STRIPS, CORES = 4, 2, 2, 2


def ctx_of(x, half, strip, core):
    return ((x * HALVES + half) * STRIPS + strip) * CORES + core


def swap_pairs():
    return [(i, i ^ 1) for i in range(32)]


def chain_pairs():
    pairs = []
    for half in range(HALVES):
        for link in range(XS * STRIPS - 1):
            a = ctx_of(link % XS, half, link // XS, 1)
            b = ctx_of((link + 1) % XS, half, (link + 1) // XS, 0)
            pairs += [(a, b), (b, a)]
    return pairs


def to_columns(tensor):
    frames, height, width, channels = tensor.shape
    shaped = tensor.reshape(height, STRIPS, XS, CORES, TILE, HALVES, channels // HALVES)
    shaped = shaped.transpose(2, 5, 1, 3, 0, 4, 6)
    return shaped.reshape(32, height * TILE, channels // HALVES)


def from_columns(arrived):
    channels = arrived.shape[-1]
    shaped = arrived.reshape(XS, HALVES, STRIPS, CORES, 8, TILE, channels)
    shaped = shaped.transpose(4, 2, 0, 3, 5, 1, 6)
    return shaped.reshape(1, 8, 64, HALVES * channels)


def mask_bias(window_mask):
    place = lax.axis_index("ctx")
    x, strip, core = place // 8, place // 2 % 2, place % 2
    col = strip * 8 + x * 2 + core
    every = lax.all_gather(window_mask, "ctx", tiled=True)
    time_blocks = every.shape[1]
    rows = jnp.stack([lax.dynamic_index_in_dim(every, col + 16 * r, 0, keepdims=False) for r in range(ROW_BLOCKS)])
    rows = rows.reshape(ROW_BLOCKS, time_blocks, 3, 3, 3) == 1
    time_pos = jnp.arange(time_blocks)
    has_left = col > 0
    has_right = col < 15
    per_query_row = []
    for rq in range(ROW_BLOCKS):
        per_dt = []
        for dt in range(3):
            inside_t = (time_pos + dt - 1 >= 0) & (time_pos + dt - 1 < time_blocks)
            per_block = []
            for block in range(3):
                per_key_row = []
                for rk in range(ROW_BLOCKS):
                    window = rows[rq, :, dt, rk - rq + 1]
                    left = window[:, 0] & has_left
                    right = window[:, 2] & has_right
                    if block == 0:
                        allowed = window[:, 1]
                        if dt == 1 and rk == rq:
                            allowed = jnp.ones_like(allowed)
                    elif block == 1:
                        allowed = jnp.where(core == 0, right, left)
                    else:
                        allowed = jnp.where(core == 0, left, right)
                    per_key_row.append(allowed & inside_t)
                per_block.append(jnp.stack(per_key_row, axis=1))
            per_dt.append(jnp.stack(per_block, axis=1))
        per_query_row.append(jnp.stack(per_dt, axis=1))
    allowed = jnp.stack(per_query_row, axis=-1).reshape(time_blocks, 18, ROW_BLOCKS)
    bias = jnp.where(allowed, 0.0, NEG_FILL).astype(jnp.float32)
    bias = jnp.broadcast_to(bias[:, :, None, :, None], (time_blocks, 18, TILE, ROW_BLOCKS, TILE * TILE))
    return bias.reshape(time_blocks, 18, BLOCK)


def grads_kernel(bias_ref, q_ref, g_ref, k0, v0, k1, v1, k2, v2, dq_ref, o0, o1, o2, a0, a1, a2):
    time_blocks = bias_ref.shape[0]
    accs = (a0, a1, a2)
    for acc in accs:
        acc[...] = jnp.zeros_like(acc)
    pairs = ((k0, v0), (k1, v1), (k2, v2))

    def one_block(t, _):
        here = pl.ds(pl.multiple_of(t * BLOCK, BLOCK), BLOCK)
        q = q_ref[here, :]
        g = g_ref[here, :]
        zero = jnp.zeros_like(q)
        both = jnp.concatenate(
            [jnp.concatenate([q, zero], axis=1), jnp.concatenate([zero, g], axis=1)], axis=0
        )
        at = []
        for dt in STEPS:
            near = jnp.clip(t + dt, 0, time_blocks - 1)
            at.append(pl.ds(pl.multiple_of(near * BLOCK, BLOCK), BLOCK))
        scores, probs, keys = [], [], []
        top = None
        for dt in range(3):
            for block, (k_ref, v_ref) in enumerate(pairs):
                k = k_ref[at[dt], :]
                kv = jnp.concatenate([k, v_ref[at[dt], :]], axis=1)
                r = lax.dot_general(kv, both, (((1,), (1,)), ((), ())), preferred_element_type=jnp.float32)
                rows = []
                for rk in range(ROW_BLOCKS):
                    row = (dt * 3 + block) * 2 + rk
                    rows.append(jnp.broadcast_to(bias_ref[t, row : row + 1, :], (16, BLOCK)))
                bias = jnp.concatenate(rows * TILE, axis=0)
                s = r[:, :BLOCK] * (SCALE * LOG2E) + bias
                here_top = jnp.max(s, axis=0, keepdims=True)
                top = here_top if top is None else jnp.maximum(top, here_top)
                scores.append(s)
                probs.append(r[:, BLOCK:])
                keys.append(k)
        total = jnp.zeros((1, BLOCK), jnp.float32)
        dots = jnp.zeros((1, BLOCK), jnp.float32)
        weights = []
        for s, pg in zip(scores, probs):
            e = jnp.exp2(s - top)
            total += jnp.sum(e, axis=0, keepdims=True)
            dots += jnp.sum(e * pg, axis=0, keepdims=True)
            weights.append(e)
        inv = 1.0 / total
        row_dot = dots * inv
        dqt = jnp.zeros((HEAD_DIM, BLOCK), jnp.float32)
        for n, (e, pg, k) in enumerate(zip(weights, probs, keys)):
            p = e * inv
            ds = (p * (pg - row_dot) * SCALE).astype(jnp.bfloat16)
            pair = jnp.concatenate([ds, p.astype(jnp.bfloat16)], axis=1)
            dkv = jnp.dot(pair, both, preferred_element_type=jnp.float32)
            dt, block = n // 3, n % 3
            accs[block][at[dt], :] += dkv
            dqt += lax.dot_general(k, ds, (((0,), (0,)), ((), ())), preferred_element_type=jnp.float32)
        dq_ref[here, :] = dqt.T.astype(jnp.bfloat16)
        return 0

    lax.fori_loop(0, time_blocks, one_block, 0)
    for acc, out in zip(accs, (o0, o1, o2)):
        out[...] = acc[...].astype(jnp.bfloat16)


def column_grads(bias, qg, own, near, far):
    rows = qg.shape[0]
    first = pl.BlockSpec((rows, HEAD_DIM), lambda h: (0, h))
    second = pl.BlockSpec((rows, HEAD_DIM), lambda h: (0, h + HEADS_LOCAL))
    pair = pl.BlockSpec((rows, 2 * HEAD_DIM), lambda h: (0, h))
    out = jax.ShapeDtypeStruct((rows, 2 * HEADS_LOCAL * HEAD_DIM), jnp.bfloat16)
    return pl.pallas_call(
        grads_kernel,
        grid=(HEADS_LOCAL,),
        in_specs=[pl.BlockSpec(bias.shape, lambda h: (0, 0, 0))] + [first, second] * 4,
        out_specs=[first, pair, pair, pair],
        out_shape=[jax.ShapeDtypeStruct((rows, HEADS_LOCAL * HEAD_DIM), jnp.bfloat16), out, out, out],
        scratch_shapes=[pltpu.VMEM((rows, 2 * HEAD_DIM), jnp.float32)] * 3,
        compiler_params=pltpu.CompilerParams(vmem_limit_bytes=48 * 1024 * 1024),
        cost_estimate=pl.CostEstimate(flops=20_000_000_000, bytes_accessed=20_000_000, transcendentals=4_000_000),
        name="column_grads",
    )(bias, qg, qg, own, own, near, near, far, far)


def shards(queries, keys, values, out_grad, window_mask):
    swap, chain = swap_pairs(), chain_pairs()
    bias = mask_bias(window_mask)
    exchange = functools.partial(lax.all_to_all, axis_name="ctx", split_axis=0, concat_axis=0, tiled=True)
    kv = exchange(jnp.concatenate([to_columns(keys), to_columns(values)], axis=-1)).reshape(1024, 768)
    near = lax.ppermute(kv, "ctx", swap)
    far = lax.ppermute(kv, "ctx", chain)
    qg = exchange(jnp.concatenate([to_columns(queries), to_columns(out_grad)], axis=-1)).reshape(1024, 768)
    dq, own, to_near, to_far = column_grads(bias, qg, kv, near, far)
    from_near = lax.ppermute(to_near, "ctx", swap)
    from_far = lax.ppermute(to_far, "ctx", chain)
    dq_back = exchange(dq.reshape(32, 32, 384))
    total = own.astype(jnp.float32) + from_near.astype(jnp.float32) + from_far.astype(jnp.float32)
    dkv_back = exchange(total.astype(jnp.bfloat16).reshape(32, 32, 768)).reshape(32, 32, 3, 2, 128)
    dk = dkv_back[:, :, :, 0].reshape(32, 32, 384)
    dv = dkv_back[:, :, :, 1].reshape(32, 32, 384)
    return from_columns(dq_back), from_columns(dk), from_columns(dv)


def solution(mesh):
    tokens = P("ctx", None, None, "head")
    return jax.shard_map(
        shards,
        mesh=mesh,
        in_specs=(tokens, tokens, tokens, tokens, P("ctx", None, None)),
        out_specs=(tokens, tokens, tokens),
        check_vma=False,
    )
```

```python
import jax
import jax.numpy as jnp
from jax import lax
from jax.experimental import pallas as pl
from jax.experimental.pallas import tpu as pltpu
from jax.sharding import PartitionSpec as P

HEAD_DIM = 128
TILE = 4
ROW_BLOCKS = 2
NEG_FILL = -1e30
SCALE = HEAD_DIM ** (-0.5)
LOG2E = 1.4426950408889634
HEADS_LOCAL = 3
BLOCK = ROW_BLOCKS * TILE**3
STEPS = (-1, 0, 1)

XS, HALVES, STRIPS, CORES = 4, 2, 2, 2


def ctx_of(x, half, strip, core):
    return ((x * HALVES + half) * STRIPS + strip) * CORES + core


def swap_pairs():
    return [(i, i ^ 1) for i in range(32)]


def mask_pairs(flip):
    pairs = []
    for row in range(ROW_BLOCKS):
        for col in range(16):
            pairs.append((row * 16 + col, ctx_of(col % 8 // 2, row ^ flip, col // 8, col % 2)))
    return pairs


def chain_pairs():
    pairs = []
    for half in range(HALVES):
        for link in range(XS * STRIPS - 1):
            a = ctx_of(link % XS, half, link // XS, 1)
            b = ctx_of((link + 1) % XS, half, (link + 1) // XS, 0)
            pairs += [(a, b), (b, a)]
    return pairs


def mask_bias(window_mask):
    place = lax.axis_index("ctx")
    x, strip, core = place // 8, place // 2 % 2, place % 2
    col = strip * 8 + x * 2 + core
    half = place // 4 % 2
    time_blocks = window_mask.shape[1]
    mine = lax.ppermute(window_mask[0], "ctx", mask_pairs(0))
    other = lax.ppermute(window_mask[0], "ctx", mask_pairs(1))
    rows = jnp.stack([jnp.where(half == 0, mine, other), jnp.where(half == 0, other, mine)])
    rows = rows.reshape(ROW_BLOCKS, time_blocks, 3, 3, 3) == 1
    time_pos = jnp.arange(time_blocks)
    has_left = col > 0
    has_right = col < 15
    per_query_row = []
    for rq in range(ROW_BLOCKS):
        per_dt = []
        for dt in range(3):
            inside_t = (time_pos + dt - 1 >= 0) & (time_pos + dt - 1 < time_blocks)
            per_block = []
            for block in range(3):
                per_key_row = []
                for rk in range(ROW_BLOCKS):
                    window = rows[rq, :, dt, rk - rq + 1]
                    left = window[:, 0] & has_left
                    right = window[:, 2] & has_right
                    if block == 0:
                        allowed = window[:, 1]
                        if dt == 1 and rk == rq:
                            allowed = jnp.ones_like(allowed)
                    elif block == 1:
                        allowed = jnp.where(core == 0, right, left)
                    else:
                        allowed = jnp.where(core == 0, left, right)
                    per_key_row.append(allowed & inside_t)
                per_block.append(jnp.stack(per_key_row, axis=1))
            per_dt.append(jnp.stack(per_block, axis=1))
        per_query_row.append(jnp.stack(per_dt, axis=1))
    allowed = jnp.stack(per_query_row, axis=-1).reshape(time_blocks, 18, ROW_BLOCKS)
    bias = jnp.where(allowed, 0.0, NEG_FILL).astype(jnp.float32)
    bias = jnp.broadcast_to(bias[:, :, None, :, None], (time_blocks, 18, TILE, ROW_BLOCKS, TILE * TILE))
    return bias.reshape(time_blocks, 18, BLOCK)


VMEM_LIMIT = 62 * 1024 * 1024


def pack_kernel(k, v, q, g, out, taken, packed, in_sems, out_sems):
    reads, writes = [], []
    for x in range(XS):
        for i, ref in enumerate((k, v, q, g)):
            reads.append(pltpu.make_async_copy(ref.at[:, :, x], taken.at[i, x], in_sems.at[x, i]))
            reads[-1].start()
    for x in range(XS):
        for i in range(4):
            reads[x * 4 + i].wait()
        for half in range(HALVES):
            for strip in range(STRIPS):
                for core in range(CORES):
                    for i in range(4):
                        for j in range(HEADS_LOCAL):
                            lane = (half * HEADS_LOCAL + j) * HEAD_DIM
                            cells = taken[i, x, :, strip, :, lane : lane + HEAD_DIM].astype(jnp.float32)
                            cells = cells[:, core * TILE : (core + 1) * TILE].reshape(32, HEAD_DIM)
                            to = ((i // 2 * HEADS_LOCAL + j) * 2 + i % 2) * HEAD_DIM
                            packed[x, half, strip, core, :, to : to + HEAD_DIM] = cells.astype(jnp.bfloat16)
            writes.append(pltpu.make_async_copy(packed.at[x, half], out.at[x, half], out_sems.at[x, half]))
            writes[-1].start()
    for write in writes:
        write.wait()


def pack(tensors):
    views = [t.reshape(8, STRIPS, XS, 8, 768) for t in tensors]
    out = (XS, HALVES, STRIPS, CORES, 32, 12 * HEAD_DIM)
    return pl.pallas_call(
        pack_kernel,
        in_specs=[pl.BlockSpec(memory_space=pl.ANY)] * 4,
        out_specs=pl.BlockSpec(memory_space=pl.ANY),
        out_shape=jax.ShapeDtypeStruct(out, jnp.bfloat16),
        scratch_shapes=[
            pltpu.VMEM((4, XS, 8, STRIPS, 8, 768), jnp.bfloat16),
            pltpu.VMEM(out, jnp.bfloat16),
            pltpu.SemaphoreType.DMA((XS, 4)),
            pltpu.SemaphoreType.DMA((XS, HALVES)),
        ],
        compiler_params=pltpu.CompilerParams(vmem_limit_bytes=VMEM_LIMIT),
        cost_estimate=pl.CostEstimate(flops=0, bytes_accessed=6_300_000, transcendentals=0),
        name="pack",
    )(*views).reshape(32, 32, 12 * HEAD_DIM)


def unpack_kernel(arrived, dk, dv, dq, taken, b0, b1, b2, in_sems, out_sems):
    reads, writes = [], []
    for x in range(XS):
        reads.append(pltpu.make_async_copy(arrived.at[x], taken.at[x], in_sems.at[x]))
        reads[-1].start()
    for x in range(XS):
        reads[x].wait()
        for i, (ref, buf) in enumerate(((dk, b0), (dv, b1), (dq, b2))):
            for strip in range(STRIPS):
                for half in range(HALVES):
                    parts = []
                    for core in range(CORES):
                        cells = taken[x, half, strip, core, :, i * 384 : (i + 1) * 384]
                        parts.append(cells.astype(jnp.float32).reshape(8, TILE, 384))
                    joined = jnp.concatenate(parts, axis=1).astype(jnp.bfloat16)
                    buf[x, :, strip, :, half * 384 : (half + 1) * 384] = joined
            writes.append(pltpu.make_async_copy(buf.at[x], ref.at[:, :, x], out_sems.at[x, i]))
            writes[-1].start()
    for write in writes:
        write.wait()


def unpack(arrived):
    out = jax.ShapeDtypeStruct((8, STRIPS, XS, 8, 768), jnp.bfloat16)
    buf = pltpu.VMEM((XS, 8, STRIPS, 8, 768), jnp.bfloat16)
    lanes = arrived.shape[-1]
    results = pl.pallas_call(
        unpack_kernel,
        in_specs=[pl.BlockSpec(memory_space=pl.ANY)],
        out_specs=[pl.BlockSpec(memory_space=pl.ANY)] * 3,
        out_shape=[out] * 3,
        scratch_shapes=[
            pltpu.VMEM((XS, HALVES, STRIPS, CORES, 32, lanes), jnp.bfloat16),
            buf,
            buf,
            buf,
            pltpu.SemaphoreType.DMA((XS,)),
            pltpu.SemaphoreType.DMA((XS, 3)),
        ],
        compiler_params=pltpu.CompilerParams(vmem_limit_bytes=VMEM_LIMIT),
        cost_estimate=pl.CostEstimate(flops=0, bytes_accessed=4_700_000, transcendentals=0),
        name="unpack",
    )(arrived.reshape(XS, HALVES, STRIPS, CORES, 32, lanes))
    return [r.reshape(1, 8, 64, 768) for r in results]


def block_bias(bias_ref, t, dt, block):
    rows = []
    for rk in range(ROW_BLOCKS):
        row = (dt * 3 + block) * 2 + rk
        rows.append(jnp.broadcast_to(bias_ref[t, row : row + 1, :], (TILE * TILE, BLOCK)))
    return jnp.concatenate(rows * TILE, axis=0)


def grads_kernel(bias_ref, qg, own, near, far, dq_ref, o0, o1, o2, a0, a1, a2):
    time_blocks = bias_ref.shape[0]
    accs, sources = (a0, a1, a2), (own, near, far)
    for acc in accs:
        acc[...] = jnp.zeros_like(acc)
    for t in range(time_blocks):
        here = pl.ds(t * BLOCK, BLOCK)
        q = qg[here, :HEAD_DIM]
        g = qg[here, HEAD_DIM:]
        zero = jnp.zeros_like(q)
        both = jnp.concatenate(
            [jnp.concatenate([q, zero], axis=1), jnp.concatenate([zero, g], axis=1)], axis=0
        )
        low, high = max(t - 1, 0), min(t + 1, time_blocks - 1)
        window = pl.ds(low * BLOCK, (high - low + 1) * BLOCK)
        scores, probs = [], []
        top = None
        for block, source in enumerate(sources):
            r = lax.dot_general(
                source[window, :], both, (((1,), (1,)), ((), ())), preferred_element_type=jnp.float32
            )
            bias = [block_bias(bias_ref, t, near_t - t + 1, block) for near_t in range(low, high + 1)]
            s = r[:, :BLOCK] * (SCALE * LOG2E) + jnp.concatenate(bias, axis=0)
            block_top = jnp.max(s, axis=0, keepdims=True)
            top = block_top if top is None else jnp.maximum(top, block_top)
            scores.append(s)
            probs.append(r[:, BLOCK:])
        total = jnp.zeros((1, BLOCK), jnp.float32)
        dots = jnp.zeros((1, BLOCK), jnp.float32)
        weights = []
        for s, pg in zip(scores, probs):
            e = jnp.exp2(s - top)
            total += jnp.sum(e, axis=0, keepdims=True)
            dots += jnp.sum(e * pg, axis=0, keepdims=True)
            weights.append(e)
        inv = 1.0 / total
        row_dot = dots * inv
        inv_scaled = inv * SCALE
        dqt = jnp.zeros((HEAD_DIM, BLOCK), jnp.float32)
        for acc, source, e, pg in zip(accs, sources, weights, probs):
            p = (e * inv).astype(jnp.bfloat16)
            ds = ((e * inv_scaled) * (pg - row_dot)).astype(jnp.bfloat16)
            pair = jnp.concatenate([ds, p], axis=1)
            acc[window, :] += jnp.dot(pair, both, preferred_element_type=jnp.float32)
            dqt += lax.dot_general(
                source[window, :HEAD_DIM], ds, (((0,), (0,)), ((), ())), preferred_element_type=jnp.float32
            )
        dq_ref[here, :] = dqt.T.astype(jnp.bfloat16)
    for acc, out in zip(accs, (o0, o1, o2)):
        out[...] = acc[...].astype(jnp.bfloat16)


def head_grads(bias, everything, near, far, head):
    rows = everything.shape[0]
    wide = (rows, 2 * HEAD_DIM)
    whole = pl.BlockSpec(wide, lambda i: (0, 0))
    out = jax.ShapeDtypeStruct(wide, jnp.bfloat16)
    return pl.pallas_call(
        grads_kernel,
        grid=(1,),
        in_specs=[
            pl.BlockSpec(bias.shape, lambda i: (0, 0, 0)),
            pl.BlockSpec(wide, lambda i: (0, HEADS_LOCAL + head)),
            pl.BlockSpec(wide, lambda i: (0, head)),
            whole,
            whole,
        ],
        out_specs=[pl.BlockSpec((rows, HEAD_DIM), lambda i: (0, 0)), whole, whole, whole],
        out_shape=[jax.ShapeDtypeStruct((rows, HEAD_DIM), jnp.bfloat16), out, out, out],
        scratch_shapes=[pltpu.VMEM(wide, jnp.float32)] * 3,
        compiler_params=pltpu.CompilerParams(vmem_limit_bytes=VMEM_LIMIT),
        cost_estimate=pl.CostEstimate(flops=7_000_000_000, bytes_accessed=4_500_000, transcendentals=1_200_000),
        name="head_grads",
    )(bias, everything, everything, near, far)


def gather_kernel(*refs):
    out = refs[-1]
    for j in range(HEADS_LOCAL):
        dq, own, near, far = refs[4 * j : 4 * j + 4]
        total = own[...].astype(jnp.float32) + near[...].astype(jnp.float32) + far[...].astype(jnp.float32)
        total = total.astype(jnp.bfloat16)
        lane = j * HEAD_DIM
        out[:, lane : lane + HEAD_DIM] = total[:, :HEAD_DIM]
        out[:, 384 + lane : 384 + lane + HEAD_DIM] = total[:, HEAD_DIM:]
        out[:, 768 + lane : 768 + lane + HEAD_DIM] = dq[...]


def gather_grads(parts):
    rows = parts[0].shape[0]
    step = rows // 4
    return pl.pallas_call(
        gather_kernel,
        grid=(4,),
        in_specs=[pl.BlockSpec((step, part.shape[1]), lambda i: (i, 0)) for part in parts],
        out_specs=pl.BlockSpec((step, 9 * HEAD_DIM), lambda i: (i, 0)),
        out_shape=jax.ShapeDtypeStruct((rows, 9 * HEAD_DIM), jnp.bfloat16),
        compiler_params=pltpu.CompilerParams(vmem_limit_bytes=VMEM_LIMIT),
        cost_estimate=pl.CostEstimate(flops=0, bytes_accessed=8_000_000, transcendentals=0),
        name="gather_grads",
    )(*parts)


def shards(queries, keys, values, out_grad, window_mask):
    swap, chain = swap_pairs(), chain_pairs()
    bias = mask_bias(window_mask)
    packed = pack((keys, values, queries, out_grad))
    everything = lax.all_to_all(packed, "ctx", 0, 0, tiled=True).reshape(1024, 12 * HEAD_DIM)
    nears, fars = [], []
    for head in range(HEADS_LOCAL):
        kv = everything[:, 2 * head * HEAD_DIM : 2 * (head + 1) * HEAD_DIM]
        nears.append(lax.ppermute(kv, "ctx", swap))
        fars.append(lax.ppermute(kv, "ctx", chain))
    parts = []
    for head in range(HEADS_LOCAL):
        dq, own, to_near, to_far = head_grads(bias, everything, nears[head], fars[head], head)
        parts += [dq, own, lax.ppermute(to_near, "ctx", swap), lax.ppermute(to_far, "ctx", chain)]
    grads = gather_grads(parts).reshape(32, 32, 9 * HEAD_DIM)
    dk, dv, dq = unpack(lax.all_to_all(grads, "ctx", 0, 0, tiled=True))
    return dq, dk, dv


def solution(mesh):
    tokens = P("ctx", None, None, "head")
    return jax.shard_map(
        shards,
        mesh=mesh,
        in_specs=(tokens, tokens, tokens, tokens, P("ctx", None, None)),
        out_specs=(tokens, tokens, tokens),
        check_vma=False,
    )
```

```python
import jax
import jax.numpy as jnp
from jax import lax
from jax.experimental import pallas as pl
from jax.experimental.pallas import tpu as pltpu
from jax.sharding import PartitionSpec as P

HEAD_DIM = 128
TILE = 4
ROW_BLOCKS = 2
NEG_FILL = -1e30
SCALE = HEAD_DIM ** (-0.5)
LOG2E = 1.4426950408889634
HEADS_LOCAL = 3
BLOCK = ROW_BLOCKS * TILE**3
STEPS = (-1, 0, 1)

XS, HALVES, STRIPS, CORES = 4, 2, 2, 2


def ctx_of(x, half, strip, core):
    return ((x * HALVES + half) * STRIPS + strip) * CORES + core


def swap_pairs():
    return [(i, i ^ 1) for i in range(32)]


def mask_pairs(flip):
    pairs = []
    for row in range(ROW_BLOCKS):
        for col in range(16):
            pairs.append((row * 16 + col, ctx_of(col % 8 // 2, row ^ flip, col // 8, col % 2)))
    return pairs


def chain_pairs():
    pairs = []
    for half in range(HALVES):
        for link in range(XS * STRIPS - 1):
            a = ctx_of(link % XS, half, link // XS, 1)
            b = ctx_of((link + 1) % XS, half, (link + 1) // XS, 0)
            pairs += [(a, b), (b, a)]
    return pairs


def mask_bias(window_mask):
    place = lax.axis_index("ctx")
    x, strip, core = place // 8, place // 2 % 2, place % 2
    col = strip * 8 + x * 2 + core
    half = place // 4 % 2
    time_blocks = window_mask.shape[1]
    mine = lax.ppermute(window_mask[0], "ctx", mask_pairs(0))
    other = lax.ppermute(window_mask[0], "ctx", mask_pairs(1))
    rows = jnp.stack([jnp.where(half == 0, mine, other), jnp.where(half == 0, other, mine)])
    rows = rows.reshape(ROW_BLOCKS, time_blocks, 3, 3, 3) == 1
    time_pos = jnp.arange(time_blocks)
    has_left = col > 0
    has_right = col < 15
    per_query_row = []
    for rq in range(ROW_BLOCKS):
        per_dt = []
        for dt in range(3):
            inside_t = (time_pos + dt - 1 >= 0) & (time_pos + dt - 1 < time_blocks)
            per_block = []
            for block in range(3):
                per_key_row = []
                for rk in range(ROW_BLOCKS):
                    window = rows[rq, :, dt, rk - rq + 1]
                    left = window[:, 0] & has_left
                    right = window[:, 2] & has_right
                    if block == 0:
                        allowed = window[:, 1]
                        if dt == 1 and rk == rq:
                            allowed = jnp.ones_like(allowed)
                    elif block == 1:
                        allowed = jnp.where(core == 0, right, left)
                    else:
                        allowed = jnp.where(core == 0, left, right)
                    per_key_row.append(allowed & inside_t)
                per_block.append(jnp.stack(per_key_row, axis=1))
            per_dt.append(jnp.stack(per_block, axis=1))
        per_query_row.append(jnp.stack(per_dt, axis=1))
    allowed = jnp.stack(per_query_row, axis=-1).reshape(time_blocks, 18, ROW_BLOCKS)
    bias = jnp.where(allowed, 0.0, NEG_FILL).astype(jnp.float32)
    bias = jnp.broadcast_to(bias[:, :, None, :, None], (time_blocks, 18, TILE, ROW_BLOCKS, TILE * TILE))
    return bias.reshape(time_blocks, 18, BLOCK)


VMEM_LIMIT = 62 * 1024 * 1024


def unpack_kernel(arrived, dk, dv, dq, taken, b0, b1, b2, in_sems, out_sems):
    reads, writes = [], []
    for x in range(XS):
        reads.append(pltpu.make_async_copy(arrived.at[x], taken.at[x], in_sems.at[x]))
        reads[-1].start()
    for x in range(XS):
        reads[x].wait()
        for i, (ref, buf) in enumerate(((dk, b0), (dv, b1), (dq, b2))):
            for strip in range(STRIPS):
                for half in range(HALVES):
                    parts = []
                    for core in range(CORES):
                        lanes = [768 + j * HEAD_DIM if i == 2 else (2 * j + i) * HEAD_DIM for j in range(HEADS_LOCAL)]
                        cells = [taken[x, half, strip, core, :, lane : lane + HEAD_DIM] for lane in lanes]
                        cells = jnp.concatenate(cells, axis=1)
                        parts.append(cells.astype(jnp.float32).reshape(8, TILE, 384))
                    joined = jnp.concatenate(parts, axis=1).astype(jnp.bfloat16)
                    buf[x, :, strip, :, half * 384 : (half + 1) * 384] = joined
            writes.append(pltpu.make_async_copy(buf.at[x], ref.at[:, :, x], out_sems.at[x, i]))
            writes[-1].start()
    for write in writes:
        write.wait()


def unpack(arrived):
    out = jax.ShapeDtypeStruct((8, STRIPS, XS, 8, 768), jnp.bfloat16)
    buf = pltpu.VMEM((XS, 8, STRIPS, 8, 768), jnp.bfloat16)
    lanes = arrived.shape[-1]
    results = pl.pallas_call(
        unpack_kernel,
        in_specs=[pl.BlockSpec(memory_space=pl.ANY)],
        out_specs=[pl.BlockSpec(memory_space=pl.ANY)] * 3,
        out_shape=[out] * 3,
        scratch_shapes=[
            pltpu.VMEM((XS, HALVES, STRIPS, CORES, 32, lanes), jnp.bfloat16),
            buf,
            buf,
            buf,
            pltpu.SemaphoreType.DMA((XS,)),
            pltpu.SemaphoreType.DMA((XS, 3)),
        ],
        compiler_params=pltpu.CompilerParams(vmem_limit_bytes=VMEM_LIMIT),
        cost_estimate=pl.CostEstimate(flops=0, bytes_accessed=4_700_000, transcendentals=0),
        name="unpack",
    )(arrived.reshape(XS, HALVES, STRIPS, CORES, 32, lanes))
    return [r.reshape(1, 8, 64, 768) for r in results]


def block_bias(bias_ref, t, dt, block):
    rows = []
    for rk in range(ROW_BLOCKS):
        row = (dt * 3 + block) * 2 + rk
        rows.append(jnp.broadcast_to(bias_ref[t, row : row + 1, :], (TILE * TILE, BLOCK)))
    return jnp.concatenate(rows * TILE, axis=0)


ANY = pl.BlockSpec(memory_space=pl.ANY)


def pack_kernel(blocks, ins, *refs):
    count = len(ins)
    inputs, out, taken, (packed, in_sems, out_sems) = refs[:count], refs[count], refs[count + 1 : -3], refs[-3:]
    reads, writes = [], []
    for x in range(XS):
        for i, (first, heads) in enumerate(ins):
            for half in range(HALVES):
                lane = (half * HEADS_LOCAL + first) * HEAD_DIM
                source = inputs[i].at[:, :, x, :, lane : lane + heads * HEAD_DIM]
                reads.append(pltpu.make_async_copy(source, taken[i].at[x, half], in_sems.at[x, i, half]))
                reads[-1].start()
    each = count * HALVES
    for x in range(XS):
        for read in reads[x * each : (x + 1) * each]:
            read.wait()
        for half in range(HALVES):
            for strip in range(STRIPS):
                for core in range(CORES):
                    for n, (i, j) in enumerate(blocks):
                        lane = (j - ins[i][0]) * HEAD_DIM
                        cells = taken[i][x, half, :, strip, :, lane : lane + HEAD_DIM].astype(jnp.float32)
                        cells = cells[:, core * TILE : (core + 1) * TILE].reshape(32, HEAD_DIM)
                        to = n * HEAD_DIM
                        packed[x, half, strip, core, :, to : to + HEAD_DIM] = cells.astype(jnp.bfloat16)
            writes.append(pltpu.make_async_copy(packed.at[x, half], out.at[x, half], out_sems.at[x, half]))
            writes[-1].start()
    for write in writes:
        write.wait()


def pack(tensors, ins, blocks, name):
    views = [t.reshape(8, STRIPS, XS, 8, 768) for t in tensors]
    out = (XS, HALVES, STRIPS, CORES, 32, len(blocks) * HEAD_DIM)
    taken = [pltpu.VMEM((XS, HALVES, 8, STRIPS, 8, heads * HEAD_DIM), jnp.bfloat16) for _, heads in ins]
    return pl.pallas_call(
        lambda *refs: pack_kernel(blocks, ins, *refs),
        in_specs=[ANY] * len(views),
        out_specs=ANY,
        out_shape=jax.ShapeDtypeStruct(out, jnp.bfloat16),
        scratch_shapes=taken
        + [
            pltpu.VMEM(out, jnp.bfloat16),
            pltpu.SemaphoreType.DMA((XS, len(ins), HALVES)),
            pltpu.SemaphoreType.DMA((XS, HALVES)),
        ],
        compiler_params=pltpu.CompilerParams(vmem_limit_bytes=VMEM_LIMIT),
        cost_estimate=pl.CostEstimate(flops=0, bytes_accessed=4_000_000, transcendentals=0),
        name=name,
    )(*views).reshape(32, 32, len(blocks) * HEAD_DIM)


def grads_kernel(lanes, *refs):
    qg_lane, own_lane, near_lane, head = lanes
    bias_ref, qg, own, near, far = refs[:5]
    grads, to_near, to_far = refs[-3:]
    time_blocks = bias_ref.shape[0]
    wide = 2 * HEAD_DIM
    sources = ((own, own_lane), (near, near_lane), (far, 0))
    mine, dq_lane = head * wide, 3 * wide + head * HEAD_DIM
    targets = ((grads, mine), (to_near, mine), (to_far, 0))
    weights, pairs = {}, {}

    def finish(tk):
        near_ts = [t for t in (tk - 1, tk, tk + 1) if 0 <= t < time_blocks]
        w = jnp.concatenate([weights[t] for t in near_ts], axis=0)
        x = [
            jnp.concatenate([pairs[t][block][tk - max(t - 1, 0)] for t in near_ts], axis=1)
            for block in range(3)
        ]
        r = jnp.dot(jnp.concatenate(x, axis=0), w, preferred_element_type=jnp.float32)
        for block, (target, lane) in enumerate(targets):
            part = r[block * BLOCK : (block + 1) * BLOCK]
            part = jnp.concatenate([part[:, :HEAD_DIM] * SCALE, part[:, HEAD_DIM:]], axis=1)
            target[pl.ds(tk * BLOCK, BLOCK), lane : lane + wide] = part.astype(jnp.bfloat16)

    for t in range(time_blocks):
        low, high = max(t - 1, 0), min(t + 1, time_blocks - 1)
        here = pl.ds(t * BLOCK, BLOCK)
        q = qg[here, qg_lane : qg_lane + HEAD_DIM]
        g = qg[here, qg_lane + HEAD_DIM : qg_lane + wide]
        zero = jnp.zeros_like(q)
        both = jnp.concatenate(
            [jnp.concatenate([q, zero], axis=1), jnp.concatenate([zero, g], axis=1)], axis=0
        )
        weights[t] = both
        window = pl.ds(low * BLOCK, (high - low + 1) * BLOCK)
        scores, probs = [], []
        top = None
        for block, (source, lane) in enumerate(sources):
            r = lax.dot_general(
                source[window, lane : lane + wide],
                both,
                (((1,), (1,)), ((), ())),
                preferred_element_type=jnp.float32,
            )
            bias = [block_bias(bias_ref, t, near_t - t + 1, block) for near_t in range(low, high + 1)]
            s = r[:, :BLOCK] * (SCALE * LOG2E) + jnp.concatenate(bias, axis=0)
            block_top = jnp.max(s, axis=0, keepdims=True)
            top = block_top if top is None else jnp.maximum(top, block_top)
            scores.append(s)
            probs.append(r[:, BLOCK:])
        total = jnp.zeros((1, BLOCK), jnp.float32)
        dots = jnp.zeros((1, BLOCK), jnp.float32)
        exps = []
        for s, pg in zip(scores, probs):
            e = jnp.exp2(s - top)
            total += jnp.sum(e, axis=0, keepdims=True)
            dots += jnp.sum(e * pg, axis=0, keepdims=True)
            exps.append(e)
        inv = 1.0 / total
        row_dot = dots * inv
        slopes, pairs[t] = [], []
        for e, pg in zip(exps, probs):
            p = e * inv
            ds = (p * (pg - row_dot)).astype(jnp.bfloat16)
            pair = jnp.concatenate([ds, p.astype(jnp.bfloat16)], axis=1)
            pairs[t].append([pair[i * BLOCK : (i + 1) * BLOCK] for i in range(high - low + 1)])
            slopes.append(ds)
        keys = [source[window, lane : lane + HEAD_DIM] for source, lane in sources]
        dq = lax.dot_general(
            jnp.concatenate(slopes, axis=0),
            jnp.concatenate(keys, axis=0),
            (((0,), (0,)), ((), ())),
            preferred_element_type=jnp.float32,
        )
        grads[here, dq_lane : dq_lane + HEAD_DIM] = (dq * SCALE).astype(jnp.bfloat16)
        if t > 0:
            finish(t - 1)
    finish(time_blocks - 1)


VMEM = pl.BlockSpec(memory_space=pltpu.VMEM)
SMALL_LIMIT = 12 * 1024 * 1024


def head_grads(bias, everything, near, far, shared, head, after):
    rows = everything.shape[0]
    wide = 2 * HEAD_DIM
    lanes = ((HEADS_LOCAL + head) * wide, head * wide, head * wide, head)
    return pl.pallas_call(
        lambda *refs: grads_kernel(lanes, *refs),
        in_specs=[VMEM] * (5 + len(shared)) + [ANY] * len(after),
        out_specs=[VMEM] * 3,
        out_shape=[
            jax.ShapeDtypeStruct((rows, 9 * HEAD_DIM), jnp.bfloat16),
            jax.ShapeDtypeStruct((rows, 6 * HEAD_DIM), jnp.bfloat16),
            jax.ShapeDtypeStruct((rows, wide), jnp.bfloat16),
        ],
        input_output_aliases={5: 0, 6: 1} if shared else {},
        compiler_params=pltpu.CompilerParams(vmem_limit_bytes=SMALL_LIMIT),
        cost_estimate=pl.CostEstimate(flops=20_000_000_000, bytes_accessed=4_500_000, transcendentals=1_200_000),
        name="head_grads",
    )(bias, everything, everything, near, far, *shared, *after)


def add_kernel(first, grads, near, *refs):
    fars, out = refs[:-1], refs[-1]
    wide = 2 * HEAD_DIM
    for j, far in enumerate(fars):
        lanes = slice((first + j) * wide, (first + j + 1) * wide)
        total = grads[:, lanes].astype(jnp.float32) + near[:, lanes].astype(jnp.float32)
        out[:, lanes] = (total + far[...].astype(jnp.float32)).astype(jnp.bfloat16)


def add_halos(grads, near, fars, first):
    return pl.pallas_call(
        lambda *refs: add_kernel(first, *refs),
        in_specs=[VMEM] * (2 + len(fars)),
        out_specs=VMEM,
        out_shape=jax.ShapeDtypeStruct(grads.shape, grads.dtype),
        input_output_aliases={0: 0},
        compiler_params=pltpu.CompilerParams(vmem_limit_bytes=SMALL_LIMIT),
        cost_estimate=pl.CostEstimate(flops=0, bytes_accessed=1000, transcendentals=0),
        name="add_halos",
    )(grads, near, *fars)


def split_kernel(arrived, bias, near, *fars):
    wide = 2 * HEAD_DIM
    for j, far in enumerate(fars):
        far[...] = arrived[:, j * wide : (j + 1) * wide]
    near[...] = arrived[:, : len(fars) * wide]


def split(arrived, bias):
    rows, wide = arrived.shape[0], 2 * HEAD_DIM
    far = jax.ShapeDtypeStruct((rows, wide), arrived.dtype)
    near = jax.ShapeDtypeStruct((rows, HEADS_LOCAL * wide), arrived.dtype)
    near, *fars = pl.pallas_call(
        split_kernel,
        in_specs=[VMEM, ANY],
        out_specs=[VMEM] * (1 + HEADS_LOCAL),
        out_shape=[near] + [far] * HEADS_LOCAL,
        compiler_params=pltpu.CompilerParams(vmem_limit_bytes=SMALL_LIMIT),
        cost_estimate=pl.CostEstimate(flops=0, bytes_accessed=1000, transcendentals=0),
        name="split",
    )(arrived, bias)
    return near, fars


def ordered(arrays, after):
    count = len(arrays)
    return pl.pallas_call(
        lambda *refs: None,
        in_specs=[VMEM] * count + [ANY],
        out_specs=[VMEM] * count,
        out_shape=[jax.ShapeDtypeStruct(array.shape, array.dtype) for array in arrays],
        input_output_aliases={i: i for i in range(count)},
        compiler_params=pltpu.CompilerParams(vmem_limit_bytes=SMALL_LIMIT),
        cost_estimate=pl.CostEstimate(flops=0, bytes_accessed=1000, transcendentals=0),
        name="ordered",
    )(*arrays, after)


def shards(queries, keys, values, out_grad, window_mask):
    swap, chain = swap_pairs(), chain_pairs()
    everything = tuple((i, j) for j in range(HEADS_LOCAL) for i in (0, 1))
    everything += tuple((i, j) for j in range(HEADS_LOCAL) for i in (2, 3))
    packed = pack((keys, values, queries, out_grad), ((0, 3),) * 4, everything, "pack")
    packed, window_mask = lax.optimization_barrier((packed, window_mask))
    arrived = lax.all_to_all(packed, "ctx", 0, 0, tiled=True).reshape(1024, 12 * HEAD_DIM)
    bias = mask_bias(window_mask)
    for_near, for_far = split(arrived, bias)
    fars = [lax.ppermute(part, "ctx", chain) for part in for_far]
    near = lax.ppermute(for_near, "ctx", swap)
    shared, back = (), []
    for j in range(HEADS_LOCAL):
        grads, to_near, to_far = head_grads(bias, arrived, near, fars[j], shared, j, back[:1] if j == 2 else [])
        shared = (grads, to_near)
        if j == 2:
            to_far, to_near = ordered((to_far, to_near), back[1])
        back.append(lax.ppermute(to_far, "ctx", chain))
    near_back = lax.ppermute(to_near, "ctx", swap)
    grads = add_halos(grads, near_back, back[:2], 0)
    grads = add_halos(grads, near_back, back[2:], 2)
    grads = lax.all_to_all(grads.reshape(32, 32, 9 * HEAD_DIM), "ctx", 0, 0, tiled=True)
    dk, dv, dq = unpack(grads)
    return dq, dk, dv


def solution(mesh):
    tokens = P("ctx", None, None, "head")
    return jax.shard_map(
        shards,
        mesh=mesh,
        in_specs=(tokens, tokens, tokens, tokens, P("ctx", None, None)),
        out_specs=(tokens, tokens, tokens),
        check_vma=False,
    )
```

```python
import jax
import jax.numpy as jnp
from jax import lax
from jax.experimental import pallas as pl
from jax.experimental.pallas import tpu as pltpu
from jax.sharding import PartitionSpec as P

HEAD_DIM = 128
TILE = 4
ROW_BLOCKS = 2
NEG_FILL = -1e30
SCALE = HEAD_DIM ** (-0.5)
LOG2E = 1.4426950408889634
HEADS_LOCAL = 3
BLOCK = ROW_BLOCKS * TILE**3
STEPS = (-1, 0, 1)

XS, HALVES, STRIPS, CORES = 4, 2, 2, 2
ORDER = (0, 3, 1, 2)


def ctx_of(x, half, strip, core):
    return ((x * HALVES + half) * STRIPS + strip) * CORES + core


def run_of(x, strip):
    return x if strip == 0 else XS - 1 - x


def swap_pairs():
    return [(i, i ^ 1) for i in range(32)]


def mask_pairs(flip):
    pairs = []
    for row in range(ROW_BLOCKS):
        for col in range(16):
            pairs.append((row * 16 + col, ctx_of(run_of(col % 8 // 2, col // 8), row ^ flip, col // 8, col % 2)))
    return pairs


def chain_pairs():
    pairs = []
    for half in range(HALVES):
        for link in range(XS * STRIPS - 1):
            a = ctx_of(run_of(link % XS, link // XS), half, link // XS, 1)
            b = ctx_of(run_of((link + 1) % XS, (link + 1) // XS), half, (link + 1) // XS, 0)
            pairs += [(a, b), (b, a)]
    return pairs


def mask_bias(window_mask):
    place = lax.axis_index("ctx")
    x, strip, core = place // 8, place // 2 % 2, place % 2
    col = strip * 8 + jnp.where(strip == 0, x, XS - 1 - x) * 2 + core
    half = place // 4 % 2
    time_blocks = window_mask.shape[1]
    mine = lax.ppermute(window_mask[0], "ctx", mask_pairs(0))
    other = lax.ppermute(window_mask[0], "ctx", mask_pairs(1))
    rows = jnp.stack([jnp.where(half == 0, mine, other), jnp.where(half == 0, other, mine)])
    rows = rows.reshape(ROW_BLOCKS, time_blocks, 3, 3, 3) == 1
    time_pos = jnp.arange(time_blocks)
    has_left = col > 0
    has_right = col < 15
    per_query_row = []
    for rq in range(ROW_BLOCKS):
        per_dt = []
        for dt in range(3):
            inside_t = (time_pos + dt - 1 >= 0) & (time_pos + dt - 1 < time_blocks)
            per_block = []
            for block in range(3):
                per_key_row = []
                for rk in range(ROW_BLOCKS):
                    window = rows[rq, :, dt, rk - rq + 1]
                    left = window[:, 0] & has_left
                    right = window[:, 2] & has_right
                    if block == 0:
                        allowed = window[:, 1]
                        if dt == 1 and rk == rq:
                            allowed = jnp.ones_like(allowed)
                    elif block == 1:
                        allowed = jnp.where(core == 0, right, left)
                    else:
                        allowed = jnp.where(core == 0, left, right)
                    per_key_row.append(allowed & inside_t)
                per_block.append(jnp.stack(per_key_row, axis=1))
            per_dt.append(jnp.stack(per_block, axis=1))
        per_query_row.append(jnp.stack(per_dt, axis=1))
    allowed = jnp.stack(per_query_row, axis=-1).reshape(time_blocks, 18, ROW_BLOCKS)
    bias = jnp.where(allowed, 0.0, NEG_FILL).astype(jnp.float32)
    bias = jnp.broadcast_to(bias[:, :, None, :, None], (time_blocks, 18, TILE, ROW_BLOCKS, TILE * TILE))
    return bias.reshape(time_blocks, 18, BLOCK)


def unpack_kernel(taken, dk, dv, dq, b0, b1, b2, out_sems):
    writes = []
    for run in ORDER:
        for i, (ref, buf) in enumerate(((dk, b0), (dv, b1), (dq, b2))):
            for strip in range(STRIPS):
                for half in range(HALVES):
                    parts = []
                    for core in range(CORES):
                        lanes = [768 + j * HEAD_DIM if i == 2 else (2 * j + i) * HEAD_DIM for j in range(HEADS_LOCAL)]
                        x = run_of(run, strip)
                        cells = [taken[x, half, strip, core, :, lane : lane + HEAD_DIM] for lane in lanes]
                        cells = jnp.concatenate(cells, axis=1)
                        parts.append(cells.astype(jnp.float32).reshape(8, TILE, 384))
                    joined = jnp.concatenate(parts, axis=1).astype(jnp.bfloat16)
                    buf[run, :, strip, :, half * 384 : (half + 1) * 384] = joined
            writes.append(pltpu.make_async_copy(buf.at[run], ref.at[:, :, run], out_sems.at[run, i]))
            writes[-1].start()
    for write in writes:
        write.wait()


def unpack(arrived):
    out = jax.ShapeDtypeStruct((8, STRIPS, XS, 8, 768), jnp.bfloat16)
    buf = pltpu.VMEM((XS, 8, STRIPS, 8, 768), jnp.bfloat16)
    lanes = arrived.shape[-1]
    results = pl.pallas_call(
        unpack_kernel,
        in_specs=[VMEM],
        out_specs=[ANY] * 3,
        out_shape=[out] * 3,
        scratch_shapes=[buf, buf, buf, pltpu.SemaphoreType.DMA((XS, 3))],
        compiler_params=pltpu.CompilerParams(vmem_limit_bytes=SMALL_LIMIT),
        cost_estimate=pl.CostEstimate(flops=0, bytes_accessed=4_700_000, transcendentals=0),
        name="unpack",
    )(arrived.reshape(XS, HALVES, STRIPS, CORES, 32, lanes))
    return [r.reshape(1, 8, 64, 768) for r in results]


def block_bias(bias_ref, t, dt, block):
    rows = []
    for rk in range(ROW_BLOCKS):
        row = (dt * 3 + block) * 2 + rk
        rows.append(jnp.broadcast_to(bias_ref[t, row : row + 1, :], (TILE * TILE, BLOCK)))
    return jnp.concatenate(rows * TILE, axis=0)


ANY = pl.BlockSpec(memory_space=pl.ANY)
VMEM = pl.BlockSpec(memory_space=pltpu.VMEM)
SMALL_LIMIT = 12 * 1024 * 1024
VMEM_LIMIT = 62 * 1024 * 1024


def pack_kernel(blocks, ins, *refs):
    count = len(ins)
    inputs, out, taken, (packed, in_sems, out_sems) = refs[:count], refs[count], refs[count + 1 : -3], refs[-3:]
    reads, writes = [], []
    for x in ORDER:
        for i, (first, heads) in enumerate(ins):
            for half in range(HALVES):
                lane = (half * HEADS_LOCAL + first) * HEAD_DIM
                source = inputs[i].at[:, :, x, :, lane : lane + heads * HEAD_DIM]
                reads.append(pltpu.make_async_copy(source, taken[i].at[x, half], in_sems.at[x, i, half]))
                reads[-1].start()
    each = count * HALVES
    for n, x in enumerate(ORDER):
        if n % 2 == 0:
            for read in reads[n * each : (n + 2) * each]:
                read.wait()
        for half in range(HALVES):
            for strip in range(STRIPS):
                for core in range(CORES):
                    for n, (i, j) in enumerate(blocks):
                        lane = (j - ins[i][0]) * HEAD_DIM
                        cells = taken[i][run_of(x, strip), half, :, strip, :, lane : lane + HEAD_DIM]
                        cells = cells.astype(jnp.float32)[:, core * TILE : (core + 1) * TILE].reshape(32, HEAD_DIM)
                        to = n * HEAD_DIM
                        packed[x, half, strip, core, :, to : to + HEAD_DIM] = cells.astype(jnp.bfloat16)
            writes.append(pltpu.make_async_copy(packed.at[x, half], out.at[x, half], out_sems.at[x, half]))
            writes[-1].start()
    for write in writes:
        write.wait()


def pack(tensors, ins, blocks, name):
    views = [t.reshape(8, STRIPS, XS, 8, 768) for t in tensors]
    out = (XS, HALVES, STRIPS, CORES, 32, len(blocks) * HEAD_DIM)
    taken = [pltpu.VMEM((XS, HALVES, 8, STRIPS, 8, heads * HEAD_DIM), jnp.bfloat16) for _, heads in ins]
    return pl.pallas_call(
        lambda *refs: pack_kernel(blocks, ins, *refs),
        in_specs=[ANY] * len(views),
        out_specs=ANY,
        out_shape=jax.ShapeDtypeStruct(out, jnp.bfloat16),
        scratch_shapes=taken
        + [
            pltpu.VMEM(out, jnp.bfloat16),
            pltpu.SemaphoreType.DMA((XS, len(ins), HALVES)),
            pltpu.SemaphoreType.DMA((XS, HALVES)),
        ],
        compiler_params=pltpu.CompilerParams(vmem_limit_bytes=VMEM_LIMIT),
        cost_estimate=pl.CostEstimate(flops=0, bytes_accessed=4_000_000, transcendentals=0),
        name=name,
    )(*views).reshape(32, 32, len(blocks) * HEAD_DIM)


def grads_kernel(lanes, onward, *refs):
    qg_lane, own_lane, near_lane, head, far_lane = lanes
    bias_ref, qg, own, near, far = refs[:5]
    grads, to_near, to_far = refs[-3 - len(onward) :][:3]
    if onward:
        refs[-1][...] = own[:, onward[0]]
    time_blocks = bias_ref.shape[0]
    wide = 2 * HEAD_DIM
    sources = ((own, own_lane), (near, near_lane), (far, 0))
    mine, dq_lane = head * wide, 3 * wide + head * HEAD_DIM
    targets = ((grads, mine), (to_near, mine), (to_far, far_lane))
    both, raw, pairs, slopes = {}, {}, {}, {}
    over_channels = (((1,), (1,)), ((), ()))

    def rows(t):
        return pl.ds(t * BLOCK, BLOCK)

    def window(t):
        low, high = max(t - 1, 0), min(t + 1, time_blocks - 1)
        return low, high, pl.ds(low * BLOCK, (high - low + 1) * BLOCK)

    def products(t):
        q = qg[rows(t), qg_lane : qg_lane + HEAD_DIM]
        g = qg[rows(t), qg_lane + HEAD_DIM : qg_lane + wide]
        zero = jnp.zeros_like(q)
        both[t] = jnp.concatenate(
            [jnp.concatenate([q, zero], axis=1), jnp.concatenate([zero, g], axis=1)], axis=0
        )
        low, high, span = window(t)
        scores, probs = [], []
        top = None
        for block, (source, lane) in enumerate(sources):
            k = source[span, lane : lane + HEAD_DIM]
            v = source[span, lane + HEAD_DIM : lane + wide]
            s = lax.dot_general(k, q, over_channels, preferred_element_type=jnp.float32)
            probs.append(lax.dot_general(v, g, over_channels, preferred_element_type=jnp.float32))
            bias = [block_bias(bias_ref, t, near_t - t + 1, block) for near_t in range(low, high + 1)]
            s = s * (SCALE * LOG2E) + jnp.concatenate(bias, axis=0)
            block_top = jnp.max(s, axis=0, keepdims=True)
            top = block_top if top is None else jnp.maximum(top, block_top)
            scores.append(s)
        raw[t] = (scores, probs, top)

    def softmax(t):
        scores, probs, top = raw.pop(t)
        low, high, _ = window(t)
        total = jnp.zeros((1, BLOCK), jnp.float32)
        dots = jnp.zeros((1, BLOCK), jnp.float32)
        exps = []
        for s, pg in zip(scores, probs):
            e = jnp.exp2(s - top)
            total += jnp.sum(e, axis=0, keepdims=True)
            dots += jnp.sum(e * pg, axis=0, keepdims=True)
            exps.append(e)
        return low, high, exps, probs, 1.0 / total, dots

    def slope(t, low, high, exps, probs, inv, dots):
        row_dot = dots * inv
        slopes[t], pairs[t] = [], []
        for e, pg in zip(exps, probs):
            p = e * inv
            ds = (p * (pg - row_dot)).astype(jnp.bfloat16)
            pair = jnp.concatenate([ds, p.astype(jnp.bfloat16)], axis=1)
            pairs[t].append([pair[i * BLOCK : (i + 1) * BLOCK] for i in range(high - low + 1)])
            slopes[t].append(ds)

    def to_query(t):
        _, _, span = window(t)
        keys = jnp.concatenate([source[span, lane : lane + HEAD_DIM] for source, lane in sources], axis=0)
        ds = jnp.concatenate(slopes.pop(t), axis=0)
        dq = lax.dot_general(ds, keys, (((0,), (0,)), ((), ())), preferred_element_type=jnp.float32)
        grads[rows(t), dq_lane : dq_lane + HEAD_DIM] = (dq * SCALE).astype(jnp.bfloat16)

    def to_keys(t):
        near_ts = [n for n in (t - 1, t, t + 1) if 0 <= n < time_blocks]
        w = jnp.concatenate([both[n] for n in near_ts], axis=0)
        x = [
            jnp.concatenate([pairs[n][block][t - max(n - 1, 0)] for n in near_ts], axis=1)
            for block in range(3)
        ]
        r = jnp.dot(jnp.concatenate(x, axis=0), w, preferred_element_type=jnp.float32)
        for block, (target, lane) in enumerate(targets):
            part = r[block * BLOCK : (block + 1) * BLOCK]
            part = jnp.concatenate([part[:, :HEAD_DIM] * SCALE, part[:, HEAD_DIM:]], axis=1)
            target[rows(t), lane : lane + wide] = part.astype(jnp.bfloat16)

    products(0)
    for t in range(time_blocks):
        if t + 1 < time_blocks:
            products(t + 1)
        if t > 1:
            to_keys(t - 2)
        state = softmax(t)
        if t > 0:
            to_query(t - 1)
        slope(t, *state)
    to_query(time_blocks - 1)
    to_keys(time_blocks - 2)
    to_keys(time_blocks - 1)


def head_grads(bias, everything, near, far, shared, head, far_lane, far_lanes, onward=()):
    rows = everything.shape[0]
    wide = 2 * HEAD_DIM
    lanes = ((HEADS_LOCAL + head) * wide, head * wide, head * wide, head, far_lane)
    return pl.pallas_call(
        lambda *refs: grads_kernel(lanes, onward, *refs),
        in_specs=[VMEM] * (5 + len(shared)),
        out_specs=[VMEM] * (3 + len(onward)),
        out_shape=[
            jax.ShapeDtypeStruct((rows, lanes_out), jnp.bfloat16)
            for lanes_out in (9 * HEAD_DIM, 6 * HEAD_DIM, far_lanes) + (wide,) * len(onward)
        ],
        input_output_aliases={5 + i: i for i in range(len(shared))},
        compiler_params=pltpu.CompilerParams(vmem_limit_bytes=SMALL_LIMIT),
        cost_estimate=pl.CostEstimate(flops=100_000_000_000, bytes_accessed=4_500_000, transcendentals=1_200_000),
        name="head_grads",
    )(bias, everything, everything, near, far, *shared)


def add_halo(grads, halo, first, flops):
    lanes = slice(first * 2 * HEAD_DIM, first * 2 * HEAD_DIM + halo.shape[1])

    def kernel(grads, halo, out):
        total = grads[:, lanes].astype(jnp.float32) + halo[...].astype(jnp.float32)
        out[:, lanes] = total.astype(jnp.bfloat16)

    return pl.pallas_call(
        kernel,
        in_specs=[VMEM] * 2,
        out_specs=VMEM,
        out_shape=jax.ShapeDtypeStruct(grads.shape, grads.dtype),
        input_output_aliases={0: 0},
        compiler_params=pltpu.CompilerParams(vmem_limit_bytes=SMALL_LIMIT),
        cost_estimate=pl.CostEstimate(flops=flops, bytes_accessed=1000, transcendentals=0),
        name="add_halo",
    )(grads, halo)


def split_kernel(arrived, bias, near, *fars):
    wide = 2 * HEAD_DIM
    for j, far in enumerate(fars):
        far[...] = arrived[:, j * wide : (j + 1) * wide]
    near[...] = arrived[:, : HEADS_LOCAL * wide]


def split(arrived, bias):
    rows, wide = arrived.shape[0], 2 * HEAD_DIM
    far = jax.ShapeDtypeStruct((rows, wide), arrived.dtype)
    near = jax.ShapeDtypeStruct((rows, HEADS_LOCAL * wide), arrived.dtype)
    near, *fars = pl.pallas_call(
        split_kernel,
        in_specs=[VMEM, ANY],
        out_specs=[VMEM] * HEADS_LOCAL,
        out_shape=[near] + [far] * (HEADS_LOCAL - 1),
        compiler_params=pltpu.CompilerParams(vmem_limit_bytes=SMALL_LIMIT),
        cost_estimate=pl.CostEstimate(flops=0, bytes_accessed=1000, transcendentals=0),
        name="split",
    )(arrived, bias)
    return near, fars


def shards(queries, keys, values, out_grad, window_mask):
    swap, chain = swap_pairs(), chain_pairs()
    wide = 2 * HEAD_DIM
    everything = tuple((i, j) for j in range(HEADS_LOCAL) for i in (0, 1))
    everything += tuple((i, j) for j in range(HEADS_LOCAL) for i in (2, 3))
    packed = pack((keys, values, queries, out_grad), ((0, 3),) * 4, everything, "pack")
    packed, window_mask = lax.optimization_barrier((packed, window_mask))
    arrived = lax.all_to_all(packed, "ctx", 0, 0, tiled=True).reshape(1024, 12 * HEAD_DIM)
    bias = mask_bias(window_mask)
    for_near, for_far = split(arrived, bias)
    fars = [lax.ppermute(part, "ctx", chain) for part in for_far]
    near = lax.ppermute(for_near, "ctx", swap)
    last = slice(2 * wide, 3 * wide)
    *shared, for_last = head_grads(bias, arrived, near, fars[0], (), 0, 0, 2 * wide, (last,))
    far = lax.ppermute(for_last, "ctx", chain)
    grads, to_near, to_far = head_grads(bias, arrived, near, fars[1], shared, 1, wide, 2 * wide)
    back = lax.ppermute(to_far, "ctx", chain)
    grads, to_near, to_far = head_grads(bias, arrived, near, far, (grads, to_near), 2, 0, wide)
    near_back = lax.ppermute(to_near, "ctx", swap)
    last_back = lax.ppermute(to_far, "ctx", chain)
    grads = add_halo(grads, back, 0, 100_000_000_000)
    grads = add_halo(grads, near_back, 0, 1000)
    grads = add_halo(grads, last_back, 2, 1000)
    grads = lax.all_to_all(grads.reshape(32, 32, 9 * HEAD_DIM), "ctx", 0, 0, tiled=True)
    dk, dv, dq = unpack(grads)
    return dq, dk, dv


def solution(mesh):
    tokens = P("ctx", None, None, "head")
    return jax.shard_map(
        shards,
        mesh=mesh,
        in_specs=(tokens, tokens, tokens, tokens, P("ctx", None, None)),
        out_specs=(tokens, tokens, tokens),
        check_vma=False,
    )
```

```python
import jax
import jax.numpy as jnp
from jax import lax
from jax.experimental import pallas as pl
from jax.experimental.pallas import tpu as pltpu
from jax.sharding import PartitionSpec as P

HEAD_DIM = 128
TILE = 4
ROW_BLOCKS = 2
NEG_FILL = -1e30
SCALE = HEAD_DIM ** (-0.5)
LOG2E = 1.4426950408889634
HEADS_LOCAL = 3
BLOCK = ROW_BLOCKS * TILE**3
STEPS = (-1, 0, 1)

XS, HALVES, STRIPS, CORES = 4, 2, 2, 2
ORDER = (0, 3, 1, 2)


def ctx_of(x, half, strip, core):
    return ((x * HALVES + half) * STRIPS + strip) * CORES + core


def run_of(x, strip):
    return x if strip == 0 else XS - 1 - x


def swap_pairs():
    return [(i, i ^ 1) for i in range(32)]


def mask_pairs(flip):
    pairs = []
    for row in range(ROW_BLOCKS):
        for col in range(16):
            pairs.append((row * 16 + col, ctx_of(run_of(col % 8 // 2, col // 8), row ^ flip, col // 8, col % 2)))
    return pairs


def chain_pairs():
    pairs = []
    for half in range(HALVES):
        for link in range(XS * STRIPS - 1):
            a = ctx_of(run_of(link % XS, link // XS), half, link // XS, 1)
            b = ctx_of(run_of((link + 1) % XS, (link + 1) // XS), half, (link + 1) // XS, 0)
            pairs += [(a, b), (b, a)]
    return pairs


def mask_bias(window_mask):
    place = lax.axis_index("ctx")
    x, strip, core = place // 8, place // 2 % 2, place % 2
    col = strip * 8 + jnp.where(strip == 0, x, XS - 1 - x) * 2 + core
    half = place // 4 % 2
    time_blocks = window_mask.shape[1]
    mine = lax.ppermute(window_mask[0], "ctx", mask_pairs(0))
    other = lax.ppermute(window_mask[0], "ctx", mask_pairs(1))
    rows = jnp.stack([jnp.where(half == 0, mine, other), jnp.where(half == 0, other, mine)])
    rows = rows.reshape(ROW_BLOCKS, time_blocks, 3, 3, 3) == 1
    time_pos = jnp.arange(time_blocks)
    has_left = col > 0
    has_right = col < 15
    per_query_row = []
    for rq in range(ROW_BLOCKS):
        per_dt = []
        for dt in range(3):
            inside_t = (time_pos + dt - 1 >= 0) & (time_pos + dt - 1 < time_blocks)
            per_block = []
            for block in range(3):
                per_key_row = []
                for rk in range(ROW_BLOCKS):
                    window = rows[rq, :, dt, rk - rq + 1]
                    left = window[:, 0] & has_left
                    right = window[:, 2] & has_right
                    if block == 0:
                        allowed = window[:, 1]
                        if dt == 1 and rk == rq:
                            allowed = jnp.ones_like(allowed)
                    elif block == 1:
                        allowed = jnp.where(core == 0, right, left)
                    else:
                        allowed = jnp.where(core == 0, left, right)
                    per_key_row.append(allowed & inside_t)
                per_block.append(jnp.stack(per_key_row, axis=1))
            per_dt.append(jnp.stack(per_block, axis=1))
        per_query_row.append(jnp.stack(per_dt, axis=1))
    allowed = jnp.stack(per_query_row, axis=-1).reshape(time_blocks, 18, ROW_BLOCKS)
    bias = jnp.where(allowed, 0.0, NEG_FILL).astype(jnp.float32)
    bias = jnp.broadcast_to(bias[:, :, None, :, None], (time_blocks, 18, TILE, ROW_BLOCKS, TILE * TILE))
    return bias.reshape(time_blocks, 18, BLOCK)


def unpack_kernel(taken, dk, dv, dq, b0, b1, b2, out_sems):
    writes = []
    for run in ORDER:
        for i, (ref, buf) in enumerate(((dk, b0), (dv, b1), (dq, b2))):
            for strip in range(STRIPS):
                for half in range(HALVES):
                    parts = []
                    for core in range(CORES):
                        lanes = [768 + j * HEAD_DIM if i == 2 else (2 * j + i) * HEAD_DIM for j in range(HEADS_LOCAL)]
                        x = run_of(run, strip)
                        cells = [taken[x, half, strip, core, :, lane : lane + HEAD_DIM] for lane in lanes]
                        cells = jnp.concatenate(cells, axis=1)
                        parts.append(cells.astype(jnp.float32).reshape(8, TILE, 384))
                    joined = jnp.concatenate(parts, axis=1).astype(jnp.bfloat16)
                    buf[run, :, strip, :, half * 384 : (half + 1) * 384] = joined
            writes.append(pltpu.make_async_copy(buf.at[run], ref.at[:, :, run], out_sems.at[run, i]))
            writes[-1].start()
    for write in writes:
        write.wait()


def unpack(arrived):
    out = jax.ShapeDtypeStruct((8, STRIPS, XS, 8, 768), jnp.bfloat16)
    buf = pltpu.VMEM((XS, 8, STRIPS, 8, 768), jnp.bfloat16)
    lanes = arrived.shape[-1]
    results = pl.pallas_call(
        unpack_kernel,
        in_specs=[VMEM],
        out_specs=[ANY] * 3,
        out_shape=[out] * 3,
        scratch_shapes=[buf, buf, buf, pltpu.SemaphoreType.DMA((XS, 3))],
        compiler_params=pltpu.CompilerParams(vmem_limit_bytes=SMALL_LIMIT),
        cost_estimate=pl.CostEstimate(flops=0, bytes_accessed=4_700_000, transcendentals=0),
        name="unpack",
    )(arrived.reshape(XS, HALVES, STRIPS, CORES, 32, lanes))
    return [r.reshape(1, 8, 64, 768) for r in results]


def block_bias(bias_ref, t, dt, block):
    rows = []
    for rk in range(ROW_BLOCKS):
        row = (dt * 3 + block) * 2 + rk
        rows.append(jnp.broadcast_to(bias_ref[t, row : row + 1, :], (TILE * TILE, BLOCK)))
    return jnp.concatenate(rows * TILE, axis=0)


ANY = pl.BlockSpec(memory_space=pl.ANY)
VMEM = pl.BlockSpec(memory_space=pltpu.VMEM)
SMALL_LIMIT = 12 * 1024 * 1024
VMEM_LIMIT = 62 * 1024 * 1024


def pack_kernel(blocks, ins, *refs):
    count = len(ins)
    inputs, out, taken, (packed, in_sems, out_sems) = refs[:count], refs[count], refs[count + 1 : -3], refs[-3:]
    reads, writes = [], []
    for x in ORDER:
        for i, (first, heads) in enumerate(ins):
            for half in range(HALVES):
                lane = (half * HEADS_LOCAL + first) * HEAD_DIM
                source = inputs[i].at[:, :, x, :, lane : lane + heads * HEAD_DIM]
                reads.append(pltpu.make_async_copy(source, taken[i].at[x, half], in_sems.at[x, i, half]))
                reads[-1].start()
    each = count * HALVES
    for n, x in enumerate(ORDER):
        if n % 2 == 0:
            for read in reads[n * each : (n + 2) * each]:
                read.wait()
        for half in range(HALVES):
            for strip in range(STRIPS):
                for core in range(CORES):
                    for n, (i, j) in enumerate(blocks):
                        lane = (j - ins[i][0]) * HEAD_DIM
                        cells = taken[i][run_of(x, strip), half, :, strip, :, lane : lane + HEAD_DIM]
                        cells = cells.astype(jnp.float32)[:, core * TILE : (core + 1) * TILE].reshape(32, HEAD_DIM)
                        to = n * HEAD_DIM
                        packed[x, half, strip, core, :, to : to + HEAD_DIM] = cells.astype(jnp.bfloat16)
            writes.append(pltpu.make_async_copy(packed.at[x, half], out.at[x, half], out_sems.at[x, half]))
            writes[-1].start()
    for write in writes:
        write.wait()


def pack(tensors, ins, blocks, name):
    views = [t.reshape(8, STRIPS, XS, 8, 768) for t in tensors]
    out = (XS, HALVES, STRIPS, CORES, 32, len(blocks) * HEAD_DIM)
    taken = [pltpu.VMEM((XS, HALVES, 8, STRIPS, 8, heads * HEAD_DIM), jnp.bfloat16) for _, heads in ins]
    return pl.pallas_call(
        lambda *refs: pack_kernel(blocks, ins, *refs),
        in_specs=[ANY] * len(views),
        out_specs=ANY,
        out_shape=jax.ShapeDtypeStruct(out, jnp.bfloat16),
        scratch_shapes=taken
        + [
            pltpu.VMEM(out, jnp.bfloat16),
            pltpu.SemaphoreType.DMA((XS, len(ins), HALVES)),
            pltpu.SemaphoreType.DMA((XS, HALVES)),
        ],
        compiler_params=pltpu.CompilerParams(vmem_limit_bytes=VMEM_LIMIT),
        cost_estimate=pl.CostEstimate(flops=0, bytes_accessed=4_000_000, transcendentals=0),
        name=name,
    )(*views).reshape(32, 32, len(blocks) * HEAD_DIM)


def grads_kernel(lanes, *refs):
    qg_lane, own_lane, near_lane, head, far_lane = lanes
    bias_ref, qg, own, near, far = refs[:5]
    grads, to_near, to_far = refs[-3:]
    time_blocks = bias_ref.shape[0]
    wide = 2 * HEAD_DIM
    sources = ((own, own_lane), (near, near_lane), (far, 0))
    mine, dq_lane = head * wide, 3 * wide + head * HEAD_DIM
    targets = ((grads, mine), (to_near, mine), (to_far, far_lane))
    both, raw, pairs, slopes = {}, {}, {}, {}
    over_channels = (((1,), (1,)), ((), ()))

    def rows(t):
        return pl.ds(t * BLOCK, BLOCK)

    def window(t):
        low, high = max(t - 1, 0), min(t + 1, time_blocks - 1)
        return low, high, pl.ds(low * BLOCK, (high - low + 1) * BLOCK)

    def products(t):
        q = qg[rows(t), qg_lane : qg_lane + HEAD_DIM]
        g = qg[rows(t), qg_lane + HEAD_DIM : qg_lane + wide]
        zero = jnp.zeros_like(q)
        both[t] = jnp.concatenate(
            [jnp.concatenate([q, zero], axis=1), jnp.concatenate([zero, g], axis=1)], axis=0
        )
        low, high, span = window(t)
        scores, probs = [], []
        top = None
        for block, (source, lane) in enumerate(sources):
            k = source[span, lane : lane + HEAD_DIM]
            v = source[span, lane + HEAD_DIM : lane + wide]
            s = lax.dot_general(k, q, over_channels, preferred_element_type=jnp.float32)
            probs.append(lax.dot_general(v, g, over_channels, preferred_element_type=jnp.float32))
            bias = [block_bias(bias_ref, t, near_t - t + 1, block) for near_t in range(low, high + 1)]
            s = s * (SCALE * LOG2E) + jnp.concatenate(bias, axis=0)
            block_top = jnp.max(s, axis=0, keepdims=True)
            top = block_top if top is None else jnp.maximum(top, block_top)
            scores.append(s)
        raw[t] = (scores, probs, top)

    def softmax(t):
        scores, probs, top = raw.pop(t)
        low, high, _ = window(t)
        total = jnp.zeros((1, BLOCK), jnp.float32)
        dots = jnp.zeros((1, BLOCK), jnp.float32)
        exps = []
        for s, pg in zip(scores, probs):
            e = jnp.exp2(s - top)
            total += jnp.sum(e, axis=0, keepdims=True)
            dots += jnp.sum(e * pg, axis=0, keepdims=True)
            exps.append(e)
        return low, high, exps, probs, 1.0 / total, dots

    def slope(t, low, high, exps, probs, inv, dots):
        row_dot = dots * inv
        slopes[t], pairs[t] = [], []
        for e, pg in zip(exps, probs):
            p = e * inv
            ds = (p * (pg - row_dot)).astype(jnp.bfloat16)
            pair = jnp.concatenate([ds, p.astype(jnp.bfloat16)], axis=1)
            pairs[t].append([pair[i * BLOCK : (i + 1) * BLOCK] for i in range(high - low + 1)])
            slopes[t].append(ds)

    def to_query(t):
        _, _, span = window(t)
        keys = jnp.concatenate([source[span, lane : lane + HEAD_DIM] for source, lane in sources], axis=0)
        ds = jnp.concatenate(slopes.pop(t), axis=0)
        dq = lax.dot_general(ds, keys, (((0,), (0,)), ((), ())), preferred_element_type=jnp.float32)
        grads[rows(t), dq_lane : dq_lane + HEAD_DIM] = (dq * SCALE).astype(jnp.bfloat16)

    def to_keys(t):
        near_ts = [n for n in (t - 1, t, t + 1) if 0 <= n < time_blocks]
        w = jnp.concatenate([both[n] for n in near_ts], axis=0)
        x = [
            jnp.concatenate([pairs[n][block][t - max(n - 1, 0)] for n in near_ts], axis=1)
            for block in range(3)
        ]
        r = jnp.dot(jnp.concatenate(x, axis=0), w, preferred_element_type=jnp.float32)
        for block, (target, lane) in enumerate(targets):
            part = r[block * BLOCK : (block + 1) * BLOCK]
            part = jnp.concatenate([part[:, :HEAD_DIM] * SCALE, part[:, HEAD_DIM:]], axis=1)
            target[rows(t), lane : lane + wide] = part.astype(jnp.bfloat16)

    products(0)
    for t in range(time_blocks):
        if t + 1 < time_blocks:
            products(t + 1)
        if t > 1:
            to_keys(t - 2)
        state = softmax(t)
        if t > 0:
            to_query(t - 1)
        slope(t, *state)
    to_query(time_blocks - 1)
    to_keys(time_blocks - 2)
    to_keys(time_blocks - 1)


def head_grads(bias, everything, near, far, shared, head, far_lane, far_lanes, flops):
    rows = everything.shape[0]
    wide = 2 * HEAD_DIM
    lanes = ((HEADS_LOCAL + head) * wide, head * wide, head * wide, head, far_lane)
    return pl.pallas_call(
        lambda *refs: grads_kernel(lanes, *refs),
        in_specs=[VMEM] * (5 + len(shared)),
        out_specs=[VMEM] * 3,
        out_shape=[
            jax.ShapeDtypeStruct((rows, lanes_out), jnp.bfloat16)
            for lanes_out in (9 * HEAD_DIM, 6 * HEAD_DIM, far_lanes)
        ],
        input_output_aliases={5 + i: i for i in range(len(shared))},
        compiler_params=pltpu.CompilerParams(vmem_limit_bytes=SMALL_LIMIT),
        cost_estimate=pl.CostEstimate(flops=flops, bytes_accessed=4_500_000, transcendentals=1_200_000),
        name="head_grads",
    )(bias, everything, everything, near, far, *shared)


def add_halo(grads, halo, first, flops):
    lanes = slice(first * 2 * HEAD_DIM, first * 2 * HEAD_DIM + halo.shape[1])

    def kernel(grads, halo, out):
        total = grads[:, lanes].astype(jnp.float32) + halo[...].astype(jnp.float32)
        out[:, lanes] = total.astype(jnp.bfloat16)

    return pl.pallas_call(
        kernel,
        in_specs=[VMEM] * 2,
        out_specs=VMEM,
        out_shape=jax.ShapeDtypeStruct(grads.shape, grads.dtype),
        input_output_aliases={0: 0},
        compiler_params=pltpu.CompilerParams(vmem_limit_bytes=SMALL_LIMIT),
        cost_estimate=pl.CostEstimate(flops=flops, bytes_accessed=1000, transcendentals=0),
        name="add_halo",
    )(grads, halo)


def split_kernel(arrived, bias, near, *fars):
    wide = 2 * HEAD_DIM
    for j, far in enumerate(fars):
        far[...] = arrived[:, j * wide : (j + 1) * wide]
    near[...] = arrived[:, : HEADS_LOCAL * wide]


def split(arrived, bias):
    rows, wide = arrived.shape[0], 2 * HEAD_DIM
    far = jax.ShapeDtypeStruct((rows, wide), arrived.dtype)
    near = jax.ShapeDtypeStruct((rows, HEADS_LOCAL * wide), arrived.dtype)
    near, *fars = pl.pallas_call(
        split_kernel,
        in_specs=[VMEM, ANY],
        out_specs=[VMEM] * HEADS_LOCAL,
        out_shape=[near] + [far] * (HEADS_LOCAL - 1),
        compiler_params=pltpu.CompilerParams(vmem_limit_bytes=SMALL_LIMIT),
        cost_estimate=pl.CostEstimate(flops=0, bytes_accessed=1000, transcendentals=0),
        name="split",
    )(arrived, bias)
    return near, fars


def take_last(arrived, after):
    rows, wide = arrived.shape[0], 2 * HEAD_DIM

    def kernel(arrived, _, out):
        out[...] = arrived[:, (HEADS_LOCAL - 1) * wide : HEADS_LOCAL * wide]

    return pl.pallas_call(
        kernel,
        in_specs=[VMEM, ANY],
        out_specs=VMEM,
        out_shape=jax.ShapeDtypeStruct((rows, wide), arrived.dtype),
        compiler_params=pltpu.CompilerParams(vmem_limit_bytes=SMALL_LIMIT),
        cost_estimate=pl.CostEstimate(flops=0, bytes_accessed=1000, transcendentals=0),
        name="take_last",
    )(arrived, after)


def shards(queries, keys, values, out_grad, window_mask):
    swap, chain = swap_pairs(), chain_pairs()
    wide = 2 * HEAD_DIM
    everything = tuple((i, j) for j in range(HEADS_LOCAL) for i in (0, 1))
    everything += tuple((i, j) for j in range(HEADS_LOCAL) for i in (2, 3))
    packed = pack((keys, values, queries, out_grad), ((0, 3),) * 4, everything, "pack")
    packed, window_mask = lax.optimization_barrier((packed, window_mask))
    arrived = lax.all_to_all(packed, "ctx", 0, 0, tiled=True).reshape(1024, 12 * HEAD_DIM)
    bias = mask_bias(window_mask)
    for_near, for_far = split(arrived, bias)
    fars = [lax.ppermute(part, "ctx", chain) for part in for_far]
    near = lax.ppermute(for_near, "ctx", swap)
    fars.append(lax.ppermute(take_last(arrived, near), "ctx", chain))
    shared = head_grads(bias, arrived, near, fars[0], (), 0, 0, 2 * wide, 1_000_000_000)
    grads, to_near, to_far = head_grads(bias, arrived, near, fars[1], shared, 1, wide, 2 * wide, 1_000_000_000)
    back = lax.ppermute(to_far, "ctx", chain)
    grads, to_near, to_far = head_grads(bias, arrived, near, fars[2], (grads, to_near), 2, 0, wide, 100_000_000_000)
    near_back = lax.ppermute(to_near, "ctx", swap)
    last_back = lax.ppermute(to_far, "ctx", chain)
    grads = add_halo(grads, back, 0, 100_000_000_000)
    grads = add_halo(grads, near_back, 0, 1000)
    grads = add_halo(grads, last_back, 2, 1000)
    grads = lax.all_to_all(grads.reshape(32, 32, 9 * HEAD_DIM), "ctx", 0, 0, tiled=True)
    dk, dv, dq = unpack(grads)
    return dq, dk, dv


def solution(mesh):
    tokens = P("ctx", None, None, "head")
    return jax.shard_map(
        shards,
        mesh=mesh,
        in_specs=(tokens, tokens, tokens, tokens, P("ctx", None, None)),
        out_specs=(tokens, tokens, tokens),
        check_vma=False,
    )
```

```python
import jax
import jax.numpy as jnp
from jax import lax
from jax.experimental import pallas as pl
from jax.experimental.pallas import tpu as pltpu
from jax.sharding import PartitionSpec as P

HEAD_DIM = 128
TILE = 4
ROW_BLOCKS = 2
NEG_FILL = -1e30
SCALE = HEAD_DIM ** (-0.5)
LOG2E = 1.4426950408889634
HEADS_LOCAL = 3
BLOCK = ROW_BLOCKS * TILE**3
STEPS = (-1, 0, 1)

XS, HALVES, STRIPS, CORES = 4, 2, 2, 2
ORDER = (0, 3, 1, 2)


def ctx_of(x, half, strip, core):
    return ((x * HALVES + half) * STRIPS + strip) * CORES + core


def run_of(x, strip):
    return x if strip == 0 else XS - 1 - x


def swap_pairs():
    return [(i, i ^ 1) for i in range(32)]


def mask_pairs(flip):
    pairs = []
    for row in range(ROW_BLOCKS):
        for col in range(16):
            pairs.append((row * 16 + col, ctx_of(run_of(col % 8 // 2, col // 8), row ^ flip, col // 8, col % 2)))
    return pairs


def chain_pairs():
    pairs = []
    for half in range(HALVES):
        for link in range(XS * STRIPS - 1):
            a = ctx_of(run_of(link % XS, link // XS), half, link // XS, 1)
            b = ctx_of(run_of((link + 1) % XS, (link + 1) // XS), half, (link + 1) // XS, 0)
            pairs += [(a, b), (b, a)]
    return pairs


def mask_bias(window_mask):
    place = lax.axis_index("ctx")
    x, strip, core = place // 8, place // 2 % 2, place % 2
    col = strip * 8 + jnp.where(strip == 0, x, XS - 1 - x) * 2 + core
    half = place // 4 % 2
    time_blocks = window_mask.shape[1]
    mine = lax.ppermute(window_mask[0], "ctx", mask_pairs(0))
    other = lax.ppermute(window_mask[0], "ctx", mask_pairs(1))
    rows = jnp.stack([jnp.where(half == 0, mine, other), jnp.where(half == 0, other, mine)])
    rows = rows.reshape(ROW_BLOCKS, time_blocks, 3, 3, 3) == 1
    time_pos = jnp.arange(time_blocks)
    has_left = col > 0
    has_right = col < 15
    per_query_row = []
    for rq in range(ROW_BLOCKS):
        per_dt = []
        for dt in range(3):
            inside_t = (time_pos + dt - 1 >= 0) & (time_pos + dt - 1 < time_blocks)
            per_block = []
            for block in range(3):
                per_key_row = []
                for rk in range(ROW_BLOCKS):
                    window = rows[rq, :, dt, rk - rq + 1]
                    left = window[:, 0] & has_left
                    right = window[:, 2] & has_right
                    if block == 0:
                        allowed = window[:, 1]
                        if dt == 1 and rk == rq:
                            allowed = jnp.ones_like(allowed)
                    elif block == 1:
                        allowed = jnp.where(core == 0, right, left)
                    else:
                        allowed = jnp.where(core == 0, left, right)
                    per_key_row.append(allowed & inside_t)
                per_block.append(jnp.stack(per_key_row, axis=1))
            per_dt.append(jnp.stack(per_block, axis=1))
        per_query_row.append(jnp.stack(per_dt, axis=1))
    allowed = jnp.stack(per_query_row, axis=-1).reshape(time_blocks, 18, ROW_BLOCKS)
    bias = jnp.where(allowed, 0.0, NEG_FILL).astype(jnp.float32)
    bias = jnp.broadcast_to(bias[:, :, None, :, None], (time_blocks, 18, TILE, ROW_BLOCKS, TILE * TILE))
    return bias.reshape(time_blocks, 18, BLOCK)


def unpack_kernel(taken, dk, dv, dq, b0, b1, b2, out_sems):
    writes = []
    for run in ORDER:
        for i, (ref, buf) in enumerate(((dk, b0), (dv, b1), (dq, b2))):
            for strip in range(STRIPS):
                for half in range(HALVES):
                    parts = []
                    for core in range(CORES):
                        lanes = [768 + j * HEAD_DIM if i == 2 else (2 * j + i) * HEAD_DIM for j in range(HEADS_LOCAL)]
                        x = run_of(run, strip)
                        cells = [taken[x, half, strip, core, :, lane : lane + HEAD_DIM] for lane in lanes]
                        cells = jnp.concatenate(cells, axis=1)
                        parts.append(cells.astype(jnp.float32).reshape(8, TILE, 384))
                    joined = jnp.concatenate(parts, axis=1).astype(jnp.bfloat16)
                    buf[run, :, strip, :, half * 384 : (half + 1) * 384] = joined
            writes.append(pltpu.make_async_copy(buf.at[run], ref.at[:, :, run], out_sems.at[run, i]))
            writes[-1].start()
    for write in writes:
        write.wait()


def unpack(arrived):
    out = jax.ShapeDtypeStruct((8, STRIPS, XS, 8, 768), jnp.bfloat16)
    buf = pltpu.VMEM((XS, 8, STRIPS, 8, 768), jnp.bfloat16)
    lanes = arrived.shape[-1]
    results = pl.pallas_call(
        unpack_kernel,
        in_specs=[VMEM],
        out_specs=[ANY] * 3,
        out_shape=[out] * 3,
        scratch_shapes=[buf, buf, buf, pltpu.SemaphoreType.DMA((XS, 3))],
        compiler_params=pltpu.CompilerParams(vmem_limit_bytes=SMALL_LIMIT),
        cost_estimate=pl.CostEstimate(flops=0, bytes_accessed=4_700_000, transcendentals=0),
        name="unpack",
    )(arrived.reshape(XS, HALVES, STRIPS, CORES, 32, lanes))
    return [r.reshape(1, 8, 64, 768) for r in results]


def block_bias(bias_ref, t, dt, block):
    rows = []
    for rk in range(ROW_BLOCKS):
        row = (dt * 3 + block) * 2 + rk
        rows.append(jnp.broadcast_to(bias_ref[t, row : row + 1, :], (TILE * TILE, BLOCK)))
    return jnp.concatenate(rows * TILE, axis=0)


ANY = pl.BlockSpec(memory_space=pl.ANY)
VMEM = pl.BlockSpec(memory_space=pltpu.VMEM)
SMALL_LIMIT = 12 * 1024 * 1024
VMEM_LIMIT = 62 * 1024 * 1024


def pack_kernel(blocks, *refs):
    inputs, out, (taken, packed, in_sems, out_sems) = refs[:-5], refs[-5], refs[-4:]
    count = len(inputs)
    reads, writes = [], []
    for x in range(XS):
        for strip in range(STRIPS):
            run = run_of(x, strip)
            for i, ref in enumerate(inputs):
                read = pltpu.make_async_copy(ref.at[:, strip, run], taken.at[i, strip, run], in_sems.at[x, strip, i])
                reads.append(read)
                read.start()
    each = count * STRIPS
    for x in range(XS):
        for read in reads[x * each : (x + 1) * each]:
            read.wait()
        for half in range(HALVES):
            for strip in range(STRIPS):
                for core in range(CORES):
                    for n, (i, j) in enumerate(blocks):
                        lane, to = (half * HEADS_LOCAL + j) * HEAD_DIM, n * HEAD_DIM
                        cells = taken[i, strip, run_of(x, strip), :, :, lane : lane + HEAD_DIM].astype(jnp.float32)
                        cells = cells[:, core * TILE : (core + 1) * TILE].reshape(32, HEAD_DIM)
                        packed[x, half, strip, core, :, to : to + HEAD_DIM] = cells.astype(jnp.bfloat16)
            writes.append(pltpu.make_async_copy(packed.at[x, half], out.at[x, half], out_sems.at[x, half]))
            writes[-1].start()
    for write in writes:
        write.wait()


def pack(tensors, blocks):
    views = [t.reshape(8, STRIPS, XS, 8, 768) for t in tensors]
    out = (XS, HALVES, STRIPS, CORES, 32, len(blocks) * HEAD_DIM)
    return pl.pallas_call(
        lambda *refs: pack_kernel(blocks, *refs),
        in_specs=[ANY] * len(views),
        out_specs=ANY,
        out_shape=jax.ShapeDtypeStruct(out, jnp.bfloat16),
        scratch_shapes=[
            pltpu.VMEM((len(views), STRIPS, XS, 8, 8, 768), jnp.bfloat16),
            pltpu.VMEM(out, jnp.bfloat16),
            pltpu.SemaphoreType.DMA((XS, STRIPS, len(views))),
            pltpu.SemaphoreType.DMA((XS, HALVES)),
        ],
        compiler_params=pltpu.CompilerParams(vmem_limit_bytes=VMEM_LIMIT),
        cost_estimate=pl.CostEstimate(flops=0, bytes_accessed=4_000_000, transcendentals=0),
        name="pack",
    )(*views).reshape(32, 32, len(blocks) * HEAD_DIM)


def grads_kernel(lanes, *refs):
    qg_lane, own_lane, near_lane, head = lanes
    bias_ref, qg, own, near, far = refs[:5]
    grads, to_near, to_far = refs[-3:]
    time_blocks = bias_ref.shape[0]
    wide = 2 * HEAD_DIM
    sources = ((own, own_lane), (near, near_lane), (far, 0))
    mine, dq_lane = head * wide, 3 * wide + head * HEAD_DIM
    targets = ((grads, mine), (to_near, mine), (to_far, 0))
    both, raw, pairs, slopes = {}, {}, {}, {}
    over_channels = (((1,), (1,)), ((), ()))

    def rows(t):
        return pl.ds(t * BLOCK, BLOCK)

    def window(t):
        low, high = max(t - 1, 0), min(t + 1, time_blocks - 1)
        return low, high, pl.ds(low * BLOCK, (high - low + 1) * BLOCK)

    def products(t):
        q = qg[rows(t), qg_lane : qg_lane + HEAD_DIM]
        g = qg[rows(t), qg_lane + HEAD_DIM : qg_lane + wide]
        zero = jnp.zeros_like(q)
        both[t] = jnp.concatenate(
            [jnp.concatenate([q, zero], axis=1), jnp.concatenate([zero, g], axis=1)], axis=0
        )
        low, high, span = window(t)
        scores, probs = [], []
        top = None
        for block, (source, lane) in enumerate(sources):
            k = source[span, lane : lane + HEAD_DIM]
            v = source[span, lane + HEAD_DIM : lane + wide]
            s = lax.dot_general(k, q, over_channels, preferred_element_type=jnp.float32)
            probs.append(lax.dot_general(v, g, over_channels, preferred_element_type=jnp.float32))
            bias = [block_bias(bias_ref, t, near_t - t + 1, block) for near_t in range(low, high + 1)]
            s = s * (SCALE * LOG2E) + jnp.concatenate(bias, axis=0)
            block_top = jnp.max(s, axis=0, keepdims=True)
            top = block_top if top is None else jnp.maximum(top, block_top)
            scores.append(s)
        raw[t] = (scores, probs, top)

    def softmax(t):
        scores, probs, top = raw.pop(t)
        low, high, _ = window(t)
        total = jnp.zeros((1, BLOCK), jnp.float32)
        dots = jnp.zeros((1, BLOCK), jnp.float32)
        exps = []
        for s, pg in zip(scores, probs):
            e = jnp.exp2(s - top)
            total += jnp.sum(e, axis=0, keepdims=True)
            dots += jnp.sum(e * pg, axis=0, keepdims=True)
            exps.append(e)
        return low, high, exps, probs, 1.0 / total, dots

    def slope(t, low, high, exps, probs, inv, dots):
        row_dot = dots * inv
        slopes[t], pairs[t] = [], []
        for e, pg in zip(exps, probs):
            p = e * inv
            ds = (p * (pg - row_dot)).astype(jnp.bfloat16)
            pair = jnp.concatenate([ds, p.astype(jnp.bfloat16)], axis=1)
            pairs[t].append([pair[i * BLOCK : (i + 1) * BLOCK] for i in range(high - low + 1)])
            slopes[t].append(ds)

    def to_query(t):
        _, _, span = window(t)
        keys = jnp.concatenate([source[span, lane : lane + HEAD_DIM] for source, lane in sources], axis=0)
        ds = jnp.concatenate(slopes.pop(t), axis=0)
        dq = lax.dot_general(ds, keys, (((0,), (0,)), ((), ())), preferred_element_type=jnp.float32)
        grads[rows(t), dq_lane : dq_lane + HEAD_DIM] = (dq * SCALE).astype(jnp.bfloat16)

    def to_keys(t):
        near_ts = [n for n in (t - 1, t, t + 1) if 0 <= n < time_blocks]
        w = jnp.concatenate([both[n] for n in near_ts], axis=0)
        x = [
            jnp.concatenate([pairs[n][block][t - max(n - 1, 0)] for n in near_ts], axis=1)
            for block in range(3)
        ]
        r = jnp.dot(jnp.concatenate(x, axis=0), w, preferred_element_type=jnp.float32)
        for block, (target, lane) in enumerate(targets):
            part = r[block * BLOCK : (block + 1) * BLOCK]
            part = jnp.concatenate([part[:, :HEAD_DIM] * SCALE, part[:, HEAD_DIM:]], axis=1)
            target[rows(t), lane : lane + wide] = part.astype(jnp.bfloat16)

    products(0)
    for t in range(time_blocks):
        if t + 1 < time_blocks:
            products(t + 1)
        if t > 1:
            to_keys(t - 2)
        state = softmax(t)
        if t > 0:
            to_query(t - 1)
        slope(t, *state)
    to_query(time_blocks - 1)
    to_keys(time_blocks - 2)
    to_keys(time_blocks - 1)


def head_grads(bias, everything, near, far, shared, head, flops, after=()):
    rows = everything.shape[0]
    wide = 2 * HEAD_DIM
    lanes = ((HEADS_LOCAL + head) * wide, head * wide, head * wide, head)
    return pl.pallas_call(
        lambda *refs: grads_kernel(lanes, *refs),
        in_specs=[VMEM] * (5 + len(shared)) + [ANY] * len(after),
        out_specs=[VMEM] * 3,
        out_shape=[
            jax.ShapeDtypeStruct((rows, lanes_out), jnp.bfloat16)
            for lanes_out in (9 * HEAD_DIM, 6 * HEAD_DIM, wide)
        ],
        input_output_aliases={5 + i: i for i in range(len(shared))},
        compiler_params=pltpu.CompilerParams(vmem_limit_bytes=SMALL_LIMIT),
        cost_estimate=pl.CostEstimate(flops=flops, bytes_accessed=4_500_000, transcendentals=1_200_000),
        name="head_grads",
    )(bias, everything, everything, near, far, *shared, *after)


def add_halo(grads, halo, first, flops):
    lanes = slice(first * 2 * HEAD_DIM, first * 2 * HEAD_DIM + halo.shape[1])

    def kernel(grads, halo, out):
        total = grads[:, lanes].astype(jnp.float32) + halo[...].astype(jnp.float32)
        out[:, lanes] = total.astype(jnp.bfloat16)

    return pl.pallas_call(
        kernel,
        in_specs=[VMEM] * 2,
        out_specs=VMEM,
        out_shape=jax.ShapeDtypeStruct(grads.shape, grads.dtype),
        input_output_aliases={0: 0},
        compiler_params=pltpu.CompilerParams(vmem_limit_bytes=SMALL_LIMIT),
        cost_estimate=pl.CostEstimate(flops=flops, bytes_accessed=1000, transcendentals=0),
        name="add_halo",
    )(grads, halo)


def split_kernel(arrived, bias, near, *fars):
    wide = 2 * HEAD_DIM
    for j, far in enumerate(fars):
        far[...] = arrived[:, j * wide : (j + 1) * wide]
    near[...] = arrived[:, : HEADS_LOCAL * wide]


def split(arrived, bias):
    rows, wide = arrived.shape[0], 2 * HEAD_DIM
    far = jax.ShapeDtypeStruct((rows, wide), arrived.dtype)
    near = jax.ShapeDtypeStruct((rows, HEADS_LOCAL * wide), arrived.dtype)
    near, *fars = pl.pallas_call(
        split_kernel,
        in_specs=[VMEM, ANY],
        out_specs=[VMEM] * HEADS_LOCAL,
        out_shape=[near] + [far] * (HEADS_LOCAL - 1),
        compiler_params=pltpu.CompilerParams(vmem_limit_bytes=SMALL_LIMIT),
        cost_estimate=pl.CostEstimate(flops=0, bytes_accessed=1000, transcendentals=0),
        name="split",
    )(arrived, bias)
    return near, fars


def take_last(arrived, after):
    rows, wide = arrived.shape[0], 2 * HEAD_DIM

    def kernel(arrived, _, out):
        out[...] = arrived[:, (HEADS_LOCAL - 1) * wide : HEADS_LOCAL * wide]

    return pl.pallas_call(
        kernel,
        in_specs=[VMEM, ANY],
        out_specs=VMEM,
        out_shape=jax.ShapeDtypeStruct((rows, wide), arrived.dtype),
        compiler_params=pltpu.CompilerParams(vmem_limit_bytes=SMALL_LIMIT),
        cost_estimate=pl.CostEstimate(flops=0, bytes_accessed=1000, transcendentals=0),
        name="take_last",
    )(arrived, after)


def shards(queries, keys, values, out_grad, window_mask):
    swap, chain = swap_pairs(), chain_pairs()
    wide = 2 * HEAD_DIM
    everything = tuple((i, j) for j in range(HEADS_LOCAL) for i in (0, 1))
    everything += tuple((i, j) for j in range(HEADS_LOCAL) for i in (2, 3))
    packed = pack((keys, values, queries, out_grad), everything)
    packed, window_mask = lax.optimization_barrier((packed, window_mask))
    arrived = lax.all_to_all(packed, "ctx", 0, 0, tiled=True).reshape(1024, 12 * HEAD_DIM)
    bias = mask_bias(window_mask)
    for_near, for_far = split(arrived, bias)
    fars = [lax.ppermute(part, "ctx", chain) for part in for_far]
    near = lax.ppermute(for_near, "ctx", swap)
    fars.append(lax.ppermute(take_last(arrived, near), "ctx", chain))
    grads, to_near, to_far = head_grads(bias, arrived, near, fars[0], (), 0, 1_000_000_000)
    back = lax.ppermute(to_far, "ctx", chain)
    grads, to_near, to_far = head_grads(bias, arrived, near, fars[1], (grads, to_near), 1, 1_000_000_000)
    next_back = lax.ppermute(to_far, "ctx", chain)
    shared = (grads, to_near)
    grads, to_near, to_far = head_grads(bias, arrived, near, fars[2], shared, 2, 3_000_000_000)
    near_back = lax.ppermute(to_near, "ctx", swap)
    last_back = lax.ppermute(to_far, "ctx", chain)
    grads = add_halo(grads, back, 0, 3_000_000_000)
    grads = add_halo(grads, next_back, 1, 100_000_000_000)
    grads = add_halo(grads, near_back, 0, 1000)
    grads = add_halo(grads, last_back, 2, 1000)
    grads = lax.all_to_all(grads.reshape(32, 32, 9 * HEAD_DIM), "ctx", 0, 0, tiled=True)
    dk, dv, dq = unpack(grads)
    return dq, dk, dv


def solution(mesh):
    tokens = P("ctx", None, None, "head")
    return jax.shard_map(
        shards,
        mesh=mesh,
        in_specs=(tokens, tokens, tokens, tokens, P("ctx", None, None)),
        out_specs=(tokens, tokens, tokens),
        check_vma=False,
    )
```

```python
import jax
import jax.numpy as jnp
from jax import lax
from jax.experimental import pallas as pl
from jax.experimental.pallas import tpu as pltpu
from jax.sharding import PartitionSpec as P

HEAD_DIM = 128
TILE = 4
ROW_BLOCKS = 2
NEG_FILL = -1e30
SCALE = HEAD_DIM ** (-0.5)
HEADS_LOCAL = 3
BLOCK = ROW_BLOCKS * TILE**3
STEPS = (-1, 0, 1)

XS, HALVES, STRIPS, CORES = 4, 2, 2, 2
ORDER = (0, 3, 1, 2)


def ctx_of(x, half, strip, core):
    return ((x * HALVES + half) * STRIPS + strip) * CORES + core


def run_of(x, strip):
    return x if strip == 0 else XS - 1 - x


def swap_pairs():
    return [(i, i ^ 1) for i in range(32)]


def mask_pairs(flip):
    pairs = []
    for row in range(ROW_BLOCKS):
        for col in range(16):
            pairs.append((row * 16 + col, ctx_of(run_of(col % 8 // 2, col // 8), row ^ flip, col // 8, col % 2)))
    return pairs


def chain_pairs():
    pairs = []
    for half in range(HALVES):
        for link in range(XS * STRIPS - 1):
            a = ctx_of(run_of(link % XS, link // XS), half, link // XS, 1)
            b = ctx_of(run_of((link + 1) % XS, (link + 1) // XS), half, (link + 1) // XS, 0)
            pairs += [(a, b), (b, a)]
    return pairs


def mask_bias(window_mask):
    place = lax.axis_index("ctx")
    x, strip, core = place // 8, place // 2 % 2, place % 2
    col = strip * 8 + jnp.where(strip == 0, x, XS - 1 - x) * 2 + core
    half = place // 4 % 2
    time_blocks = window_mask.shape[1]
    mine = lax.ppermute(window_mask[0], "ctx", mask_pairs(0))
    other = lax.ppermute(window_mask[0], "ctx", mask_pairs(1))
    rows = jnp.stack([jnp.where(half == 0, mine, other), jnp.where(half == 0, other, mine)])
    rows = rows.reshape(ROW_BLOCKS, time_blocks, 3, 3, 3) == 1
    time_pos = jnp.arange(time_blocks)
    has_left = col > 0
    has_right = col < 15
    per_query_row = []
    for rq in range(ROW_BLOCKS):
        per_dt = []
        for dt in range(3):
            inside_t = (time_pos + dt - 1 >= 0) & (time_pos + dt - 1 < time_blocks)
            per_block = []
            for block in range(3):
                per_key_row = []
                for rk in range(ROW_BLOCKS):
                    window = rows[rq, :, dt, rk - rq + 1]
                    left = window[:, 0] & has_left
                    right = window[:, 2] & has_right
                    if block == 0:
                        allowed = window[:, 1]
                        if dt == 1 and rk == rq:
                            allowed = jnp.ones_like(allowed)
                    elif block == 1:
                        allowed = jnp.where(core == 0, right, left)
                    else:
                        allowed = jnp.where(core == 0, left, right)
                    per_key_row.append(allowed & inside_t)
                per_block.append(jnp.stack(per_key_row, axis=1))
            per_dt.append(jnp.stack(per_block, axis=1))
        per_query_row.append(jnp.stack(per_dt, axis=1))
    allowed = jnp.stack(per_query_row, axis=-1).reshape(time_blocks, 18, ROW_BLOCKS)
    bias = jnp.where(allowed, 0.0, NEG_FILL).astype(jnp.float32)
    bias = jnp.broadcast_to(bias[:, :, None, :, None], (time_blocks, 18, TILE, ROW_BLOCKS, TILE * TILE))
    return bias.reshape(time_blocks, 18, BLOCK)


def unpack_kernel(taken, dk, dv, dq, b0, b1, b2, out_sems):
    writes = []
    for run in ORDER:
        for i, (ref, buf) in enumerate(((dk, b0), (dv, b1), (dq, b2))):
            for strip in range(STRIPS):
                for half in range(HALVES):
                    parts = []
                    for core in range(CORES):
                        lanes = [768 + j * HEAD_DIM if i == 2 else (2 * j + i) * HEAD_DIM for j in range(HEADS_LOCAL)]
                        x = run_of(run, strip)
                        cells = [taken[x, half, strip, core, :, lane : lane + HEAD_DIM] for lane in lanes]
                        cells = jnp.concatenate(cells, axis=1)
                        parts.append(cells.astype(jnp.float32).reshape(8, TILE, 384))
                    joined = jnp.concatenate(parts, axis=1).astype(jnp.bfloat16)
                    buf[run, :, strip, :, half * 384 : (half + 1) * 384] = joined
            writes.append(pltpu.make_async_copy(buf.at[run], ref.at[:, :, run], out_sems.at[run, i]))
            writes[-1].start()
    for write in writes:
        write.wait()


def unpack(arrived):
    out = jax.ShapeDtypeStruct((8, STRIPS, XS, 8, 768), jnp.bfloat16)
    buf = pltpu.VMEM((XS, 8, STRIPS, 8, 768), jnp.bfloat16)
    lanes = arrived.shape[-1]
    results = pl.pallas_call(
        unpack_kernel,
        in_specs=[VMEM],
        out_specs=[ANY] * 3,
        out_shape=[out] * 3,
        scratch_shapes=[buf, buf, buf, pltpu.SemaphoreType.DMA((XS, 3))],
        compiler_params=pltpu.CompilerParams(vmem_limit_bytes=SMALL_LIMIT),
        cost_estimate=pl.CostEstimate(flops=0, bytes_accessed=4_700_000, transcendentals=0),
        name="unpack",
    )(arrived.reshape(XS, HALVES, STRIPS, CORES, 32, lanes))
    return [r.reshape(1, 8, 64, 768) for r in results]


def block_bias(bias_ref, t, dt, block):
    rows = []
    for rk in range(ROW_BLOCKS):
        row = (dt * 3 + block) * 2 + rk
        rows.append(jnp.broadcast_to(bias_ref[t, row : row + 1, :], (TILE * TILE, BLOCK)))
    return jnp.concatenate(rows * TILE, axis=0)


ANY = pl.BlockSpec(memory_space=pl.ANY)
VMEM = pl.BlockSpec(memory_space=pltpu.VMEM)
SMALL_LIMIT = 12 * 1024 * 1024
VMEM_LIMIT = 62 * 1024 * 1024


def pack_kernel(blocks, *refs):
    inputs, out, (taken, packed, in_sems, out_sems) = refs[:-5], refs[-5], refs[-4:]
    count = len(inputs)
    reads, writes = [], []
    for x in range(XS):
        for strip in range(STRIPS):
            run = run_of(x, strip)
            for i, ref in enumerate(inputs):
                read = pltpu.make_async_copy(ref.at[:, strip, run], taken.at[i, strip, run], in_sems.at[x, strip, i])
                reads.append(read)
                read.start()
    each = count * STRIPS
    for x in range(XS):
        for read in reads[x * each : (x + 1) * each]:
            read.wait()
        for half in range(HALVES):
            for strip in range(STRIPS):
                for core in range(CORES):
                    for n, (i, j) in enumerate(blocks):
                        lane, to = (half * HEADS_LOCAL + j) * HEAD_DIM, n * HEAD_DIM
                        cells = taken[i, strip, run_of(x, strip), :, :, lane : lane + HEAD_DIM].astype(jnp.float32)
                        cells = cells[:, core * TILE : (core + 1) * TILE].reshape(32, HEAD_DIM)
                        packed[x, half, strip, core, :, to : to + HEAD_DIM] = cells.astype(jnp.bfloat16)
            writes.append(pltpu.make_async_copy(packed.at[x, half], out.at[x, half], out_sems.at[x, half]))
            writes[-1].start()
    for write in writes:
        write.wait()


def pack(tensors, blocks):
    views = [t.reshape(8, STRIPS, XS, 8, 768) for t in tensors]
    out = (XS, HALVES, STRIPS, CORES, 32, len(blocks) * HEAD_DIM)
    return pl.pallas_call(
        lambda *refs: pack_kernel(blocks, *refs),
        in_specs=[ANY] * len(views),
        out_specs=ANY,
        out_shape=jax.ShapeDtypeStruct(out, jnp.bfloat16),
        scratch_shapes=[
            pltpu.VMEM((len(views), STRIPS, XS, 8, 8, 768), jnp.bfloat16),
            pltpu.VMEM(out, jnp.bfloat16),
            pltpu.SemaphoreType.DMA((XS, STRIPS, len(views))),
            pltpu.SemaphoreType.DMA((XS, HALVES)),
        ],
        compiler_params=pltpu.CompilerParams(vmem_limit_bytes=VMEM_LIMIT),
        cost_estimate=pl.CostEstimate(flops=0, bytes_accessed=4_000_000, transcendentals=0),
        name="pack",
    )(*views).reshape(32, 32, len(blocks) * HEAD_DIM)


def grads_kernel(lanes, *refs):
    qg_lane, own_lane, near_lane, head = lanes
    bias_ref, qg, own, near, far = refs[:5]
    grads, to_near, to_far = refs[-3:]
    time_blocks = bias_ref.shape[0]
    wide = 2 * HEAD_DIM
    sources = ((own, own_lane), (near, near_lane), (far, 0))
    mine, dq_lane = head * wide, 3 * wide + head * HEAD_DIM
    targets = ((grads, mine), (to_near, mine), (to_far, 0))
    both, raw, pairs, slopes = {}, {}, {}, {}
    over_channels = (((1,), (1,)), ((), ()))

    def rows(t):
        return pl.ds(t * BLOCK, BLOCK)

    def window(t):
        low, high = max(t - 1, 0), min(t + 1, time_blocks - 1)
        return low, high, pl.ds(low * BLOCK, (high - low + 1) * BLOCK)

    def products(t):
        q = qg[rows(t), qg_lane : qg_lane + HEAD_DIM]
        g = qg[rows(t), qg_lane + HEAD_DIM : qg_lane + wide]
        zero = jnp.zeros_like(q)
        both[t] = jnp.concatenate(
            [jnp.concatenate([q, zero], axis=1), jnp.concatenate([zero, g], axis=1)], axis=0
        )
        low, high, span = window(t)
        scores, probs = [], []
        top = None
        for block, (source, lane) in enumerate(sources):
            k = source[span, lane : lane + HEAD_DIM]
            v = source[span, lane + HEAD_DIM : lane + wide]
            s = lax.dot_general(k, q, over_channels, preferred_element_type=jnp.float32)
            probs.append(lax.dot_general(v, g, over_channels, preferred_element_type=jnp.float32))
            bias = [block_bias(bias_ref, t, near_t - t + 1, block) for near_t in range(low, high + 1)]
            s = s * SCALE + jnp.concatenate(bias, axis=0)
            block_top = jnp.max(s, axis=0, keepdims=True)
            top = block_top if top is None else jnp.maximum(top, block_top)
            scores.append(s)
        raw[t] = (scores, probs, top)

    def softmax(t):
        scores, probs, top = raw.pop(t)
        low, high, _ = window(t)
        total = jnp.zeros((1, BLOCK), jnp.float32)
        exps = []
        for s in scores:
            e = jnp.exp(s - top)
            total += jnp.sum(e, axis=0, keepdims=True)
            exps.append(e)
        inv = 1.0 / total
        row_dot = jnp.zeros((1, BLOCK), jnp.float32)
        lows = []
        for e, pg in zip(exps, probs):
            lows.append((e * inv).astype(jnp.bfloat16))
            row_dot += jnp.sum(lows[-1].astype(jnp.float32) * pg, axis=0, keepdims=True)
        return low, high, exps, probs, inv, row_dot, lows

    def slope(t, low, high, exps, probs, inv, row_dot, lows):
        slopes[t], pairs[t] = [], []
        for e, pg, p in zip(exps, probs, lows):
            ds = ((e * inv) * (pg - row_dot) * SCALE).astype(jnp.bfloat16)
            pair = jnp.concatenate([ds, p], axis=1)
            pairs[t].append([pair[i * BLOCK : (i + 1) * BLOCK] for i in range(high - low + 1)])
            slopes[t].append(ds)

    def to_query(t):
        _, _, span = window(t)
        keys = jnp.concatenate([source[span, lane : lane + HEAD_DIM] for source, lane in sources], axis=0)
        ds = jnp.concatenate(slopes.pop(t), axis=0)
        dq = lax.dot_general(ds, keys, (((0,), (0,)), ((), ())), preferred_element_type=jnp.float32)
        grads[rows(t), dq_lane : dq_lane + HEAD_DIM] = dq.astype(jnp.bfloat16)

    def to_keys(t):
        near_ts = [n for n in (t - 1, t, t + 1) if 0 <= n < time_blocks]
        w = jnp.concatenate([both[n] for n in near_ts], axis=0)
        x = [
            jnp.concatenate([pairs[n][block][t - max(n - 1, 0)] for n in near_ts], axis=1)
            for block in range(3)
        ]
        r = jnp.dot(jnp.concatenate(x, axis=0), w, preferred_element_type=jnp.float32)
        for block, (target, lane) in enumerate(targets):
            part = r[block * BLOCK : (block + 1) * BLOCK]
            target[rows(t), lane : lane + wide] = part.astype(jnp.bfloat16)

    products(0)
    for t in range(time_blocks):
        if t + 1 < time_blocks:
            products(t + 1)
        if t > 1:
            to_keys(t - 2)
        state = softmax(t)
        if t > 0:
            to_query(t - 1)
        slope(t, *state)
    to_query(time_blocks - 1)
    to_keys(time_blocks - 2)
    to_keys(time_blocks - 1)


def head_grads(bias, everything, near, far, shared, head, flops, after=()):
    rows = everything.shape[0]
    wide = 2 * HEAD_DIM
    lanes = ((HEADS_LOCAL + head) * wide, head * wide, head * wide, head)
    return pl.pallas_call(
        lambda *refs: grads_kernel(lanes, *refs),
        in_specs=[VMEM] * (5 + len(shared)) + [ANY] * len(after),
        out_specs=[VMEM] * 3,
        out_shape=[
            jax.ShapeDtypeStruct((rows, lanes_out), jnp.bfloat16)
            for lanes_out in (9 * HEAD_DIM, 6 * HEAD_DIM, wide)
        ],
        input_output_aliases={5 + i: i for i in range(len(shared))},
        compiler_params=pltpu.CompilerParams(vmem_limit_bytes=SMALL_LIMIT),
        cost_estimate=pl.CostEstimate(flops=flops, bytes_accessed=4_500_000, transcendentals=1_200_000),
        name="head_grads",
    )(bias, everything, everything, near, far, *shared, *after)


def add_halo(grads, halo, first, flops):
    lanes = slice(first * 2 * HEAD_DIM, first * 2 * HEAD_DIM + halo.shape[1])

    def kernel(grads, halo, out):
        total = grads[:, lanes].astype(jnp.float32) + halo[...].astype(jnp.float32)
        out[:, lanes] = total.astype(jnp.bfloat16)

    return pl.pallas_call(
        kernel,
        in_specs=[VMEM] * 2,
        out_specs=VMEM,
        out_shape=jax.ShapeDtypeStruct(grads.shape, grads.dtype),
        input_output_aliases={0: 0},
        compiler_params=pltpu.CompilerParams(vmem_limit_bytes=SMALL_LIMIT),
        cost_estimate=pl.CostEstimate(flops=flops, bytes_accessed=1000, transcendentals=0),
        name="add_halo",
    )(grads, halo)


def split_kernel(arrived, bias, near, *fars):
    wide = 2 * HEAD_DIM
    for j, far in enumerate(fars):
        far[...] = arrived[:, j * wide : (j + 1) * wide]
    near[...] = arrived[:, : HEADS_LOCAL * wide]


def split(arrived, bias):
    rows, wide = arrived.shape[0], 2 * HEAD_DIM
    far = jax.ShapeDtypeStruct((rows, wide), arrived.dtype)
    near = jax.ShapeDtypeStruct((rows, HEADS_LOCAL * wide), arrived.dtype)
    near, *fars = pl.pallas_call(
        split_kernel,
        in_specs=[VMEM, ANY],
        out_specs=[VMEM] * HEADS_LOCAL,
        out_shape=[near] + [far] * (HEADS_LOCAL - 1),
        compiler_params=pltpu.CompilerParams(vmem_limit_bytes=SMALL_LIMIT),
        cost_estimate=pl.CostEstimate(flops=0, bytes_accessed=1000, transcendentals=0),
        name="split",
    )(arrived, bias)
    return near, fars


def take_last(arrived, after):
    rows, wide = arrived.shape[0], 2 * HEAD_DIM

    def kernel(arrived, _, out):
        out[...] = arrived[:, (HEADS_LOCAL - 1) * wide : HEADS_LOCAL * wide]

    return pl.pallas_call(
        kernel,
        in_specs=[VMEM, ANY],
        out_specs=VMEM,
        out_shape=jax.ShapeDtypeStruct((rows, wide), arrived.dtype),
        compiler_params=pltpu.CompilerParams(vmem_limit_bytes=SMALL_LIMIT),
        cost_estimate=pl.CostEstimate(flops=0, bytes_accessed=1000, transcendentals=0),
        name="take_last",
    )(arrived, after)


def shards(queries, keys, values, out_grad, window_mask):
    swap, chain = swap_pairs(), chain_pairs()
    wide = 2 * HEAD_DIM
    everything = tuple((i, j) for j in range(HEADS_LOCAL) for i in (0, 1))
    everything += tuple((i, j) for j in range(HEADS_LOCAL) for i in (2, 3))
    packed = pack((keys, values, queries, out_grad), everything)
    packed, window_mask = lax.optimization_barrier((packed, window_mask))
    arrived = lax.all_to_all(packed, "ctx", 0, 0, tiled=True).reshape(1024, 12 * HEAD_DIM)
    bias = mask_bias(window_mask)
    for_near, for_far = split(arrived, bias)
    fars = [lax.ppermute(part, "ctx", chain) for part in for_far]
    near = lax.ppermute(for_near, "ctx", swap)
    fars.append(lax.ppermute(take_last(arrived, near), "ctx", chain))
    grads, to_near, to_far = head_grads(bias, arrived, near, fars[0], (), 0, 1_000_000_000)
    back = lax.ppermute(to_far, "ctx", chain)
    grads, to_near, to_far = head_grads(bias, arrived, near, fars[1], (grads, to_near), 1, 1_000_000_000)
    next_back = lax.ppermute(to_far, "ctx", chain)
    shared = (grads, to_near)
    grads, to_near, to_far = head_grads(bias, arrived, near, fars[2], shared, 2, 3_000_000_000)
    near_back = lax.ppermute(to_near, "ctx", swap)
    last_back = lax.ppermute(to_far, "ctx", chain)
    grads = add_halo(grads, back, 0, 3_000_000_000)
    grads = add_halo(grads, next_back, 1, 100_000_000_000)
    grads = add_halo(grads, near_back, 0, 1000)
    grads = add_halo(grads, last_back, 2, 1000)
    grads = lax.all_to_all(grads.reshape(32, 32, 9 * HEAD_DIM), "ctx", 0, 0, tiled=True)
    dk, dv, dq = unpack(grads)
    return dq, dk, dv


def solution(mesh):
    tokens = P("ctx", None, None, "head")
    return jax.shard_map(
        shards,
        mesh=mesh,
        in_specs=(tokens, tokens, tokens, tokens, P("ctx", None, None)),
        out_specs=(tokens, tokens, tokens),
        check_vma=False,
    )
```

```python
import jax
import jax.numpy as jnp
from jax import lax
from jax.experimental import pallas as pl
from jax.experimental.pallas import tpu as pltpu
from jax.sharding import PartitionSpec as P

HEAD_DIM = 128
TILE = 4
ROW_BLOCKS = 2
NEG_FILL = -1e30
SCALE = HEAD_DIM ** (-0.5)
HEADS_LOCAL = 3
BLOCK = ROW_BLOCKS * TILE**3
STEPS = (-1, 0, 1)

XS, HALVES, STRIPS, CORES = 4, 2, 2, 2
ORDER = (0, 3, 1, 2)


def ctx_of(x, half, strip, core):
    return ((x * HALVES + half) * STRIPS + strip) * CORES + core


def run_of(x, strip):
    return x if strip == 0 else XS - 1 - x


def swap_pairs():
    return [(i, i ^ 1) for i in range(32)]


def mask_pairs(flip):
    pairs = []
    for row in range(ROW_BLOCKS):
        for col in range(16):
            pairs.append((row * 16 + col, ctx_of(run_of(col % 8 // 2, col // 8), row ^ flip, col // 8, col % 2)))
    return pairs


def chain_pairs():
    pairs = []
    for half in range(HALVES):
        for link in range(XS * STRIPS - 1):
            a = ctx_of(run_of(link % XS, link // XS), half, link // XS, 1)
            b = ctx_of(run_of((link + 1) % XS, (link + 1) // XS), half, (link + 1) // XS, 0)
            pairs += [(a, b), (b, a)]
    return pairs


def mask_bias(window_mask):
    place = lax.axis_index("ctx")
    x, strip, core = place // 8, place // 2 % 2, place % 2
    col = strip * 8 + jnp.where(strip == 0, x, XS - 1 - x) * 2 + core
    half = place // 4 % 2
    time_blocks = window_mask.shape[1]
    mine = lax.ppermute(window_mask[0], "ctx", mask_pairs(0))
    other = lax.ppermute(window_mask[0], "ctx", mask_pairs(1))
    rows = jnp.stack([jnp.where(half == 0, mine, other), jnp.where(half == 0, other, mine)])
    rows = rows.reshape(ROW_BLOCKS, time_blocks, 3, 3, 3) == 1
    time_pos = jnp.arange(time_blocks)
    has_left = col > 0
    has_right = col < 15
    per_query_row = []
    for rq in range(ROW_BLOCKS):
        per_dt = []
        for dt in range(3):
            inside_t = (time_pos + dt - 1 >= 0) & (time_pos + dt - 1 < time_blocks)
            per_block = []
            for block in range(3):
                per_key_row = []
                for rk in range(ROW_BLOCKS):
                    window = rows[rq, :, dt, rk - rq + 1]
                    left = window[:, 0] & has_left
                    right = window[:, 2] & has_right
                    if block == 0:
                        allowed = window[:, 1]
                        if dt == 1 and rk == rq:
                            allowed = jnp.ones_like(allowed)
                    elif block == 1:
                        allowed = jnp.where(core == 0, right, left)
                    else:
                        allowed = jnp.where(core == 0, left, right)
                    per_key_row.append(allowed & inside_t)
                per_block.append(jnp.stack(per_key_row, axis=1))
            per_dt.append(jnp.stack(per_block, axis=1))
        per_query_row.append(jnp.stack(per_dt, axis=1))
    allowed = jnp.stack(per_query_row, axis=-1).reshape(time_blocks, 18, ROW_BLOCKS)
    bias = jnp.where(allowed, 0.0, NEG_FILL).astype(jnp.float32)
    bias = jnp.broadcast_to(bias[:, :, None, :, None], (time_blocks, 18, TILE, ROW_BLOCKS, TILE * TILE))
    return bias.reshape(time_blocks, 18, BLOCK)


def unpack_kernel(taken, dk, dv, dq, b0, b1, b2, out_sems):
    writes = []
    for run in ORDER:
        for i, (ref, buf) in enumerate(((dk, b0), (dv, b1), (dq, b2))):
            for strip in range(STRIPS):
                for half in range(HALVES):
                    parts = []
                    for core in range(CORES):
                        lanes = [768 + j * HEAD_DIM if i == 2 else (2 * j + i) * HEAD_DIM for j in range(HEADS_LOCAL)]
                        x = run_of(run, strip)
                        cells = [taken[x, half, strip, core, :, lane : lane + HEAD_DIM] for lane in lanes]
                        cells = jnp.concatenate(cells, axis=1)
                        parts.append(cells.astype(jnp.float32).reshape(8, TILE, 384))
                    joined = jnp.concatenate(parts, axis=1).astype(jnp.bfloat16)
                    buf[run, :, strip, :, half * 384 : (half + 1) * 384] = joined
            writes.append(pltpu.make_async_copy(buf.at[run], ref.at[:, :, run], out_sems.at[run, i]))
            writes[-1].start()
    for write in writes:
        write.wait()


def unpack(arrived):
    out = jax.ShapeDtypeStruct((8, STRIPS, XS, 8, 768), jnp.bfloat16)
    buf = pltpu.VMEM((XS, 8, STRIPS, 8, 768), jnp.bfloat16)
    lanes = arrived.shape[-1]
    results = pl.pallas_call(
        unpack_kernel,
        in_specs=[VMEM],
        out_specs=[ANY] * 3,
        out_shape=[out] * 3,
        scratch_shapes=[buf, buf, buf, pltpu.SemaphoreType.DMA((XS, 3))],
        compiler_params=pltpu.CompilerParams(vmem_limit_bytes=SMALL_LIMIT),
        cost_estimate=pl.CostEstimate(flops=0, bytes_accessed=4_700_000, transcendentals=0),
        name="unpack",
    )(arrived.reshape(XS, HALVES, STRIPS, CORES, 32, lanes))
    return [r.reshape(1, 8, 64, 768) for r in results]


def block_bias(bias_ref, t, dt, block):
    rows = []
    for rk in range(ROW_BLOCKS):
        row = (dt * 3 + block) * 2 + rk
        rows.append(jnp.broadcast_to(bias_ref[t, row : row + 1, :], (TILE * TILE, BLOCK)))
    return jnp.concatenate(rows * TILE, axis=0)


ANY = pl.BlockSpec(memory_space=pl.ANY)
VMEM = pl.BlockSpec(memory_space=pltpu.VMEM)
SMALL_LIMIT = 12 * 1024 * 1024
VMEM_LIMIT = 62 * 1024 * 1024


def pack_kernel(blocks, *refs):
    inputs, out, (taken, packed, in_sems, out_sems) = refs[:-5], refs[-5], refs[-4:]
    count = len(inputs)
    reads, writes = [], []
    for x in range(XS):
        for strip in range(STRIPS):
            run = run_of(x, strip)
            for i, ref in enumerate(inputs):
                read = pltpu.make_async_copy(ref.at[:, strip, run], taken.at[i, strip, run], in_sems.at[x, strip, i])
                reads.append(read)
                read.start()
    each = count * STRIPS
    for x in range(XS):
        for read in reads[x * each : (x + 1) * each]:
            read.wait()
        for half in range(HALVES):
            for strip in range(STRIPS):
                for core in range(CORES):
                    for n, (i, j) in enumerate(blocks):
                        lane, to = (half * HEADS_LOCAL + j) * HEAD_DIM, n * HEAD_DIM
                        cells = taken[i, strip, run_of(x, strip), :, :, lane : lane + HEAD_DIM].astype(jnp.float32)
                        cells = cells[:, core * TILE : (core + 1) * TILE].reshape(32, HEAD_DIM)
                        packed[x, half, strip, core, :, to : to + HEAD_DIM] = cells.astype(jnp.bfloat16)
            writes.append(pltpu.make_async_copy(packed.at[x, half], out.at[x, half], out_sems.at[x, half]))
            writes[-1].start()
    for write in writes:
        write.wait()


def pack(tensors, blocks):
    views = [t.reshape(8, STRIPS, XS, 8, 768) for t in tensors]
    out = (XS, HALVES, STRIPS, CORES, 32, len(blocks) * HEAD_DIM)
    return pl.pallas_call(
        lambda *refs: pack_kernel(blocks, *refs),
        in_specs=[ANY] * len(views),
        out_specs=ANY,
        out_shape=jax.ShapeDtypeStruct(out, jnp.bfloat16),
        scratch_shapes=[
            pltpu.VMEM((len(views), STRIPS, XS, 8, 8, 768), jnp.bfloat16),
            pltpu.VMEM(out, jnp.bfloat16),
            pltpu.SemaphoreType.DMA((XS, STRIPS, len(views))),
            pltpu.SemaphoreType.DMA((XS, HALVES)),
        ],
        compiler_params=pltpu.CompilerParams(vmem_limit_bytes=VMEM_LIMIT),
        cost_estimate=pl.CostEstimate(flops=0, bytes_accessed=4_000_000, transcendentals=0),
        name="pack",
    )(*views).reshape(32, 32, len(blocks) * HEAD_DIM)


def grads_kernel(lanes, *refs):
    qg_lane, own_lane, near_lane, head = lanes
    bias_ref, qg, own, near, far = refs[:5]
    grads, to_near, to_far = refs[-3:]
    time_blocks = bias_ref.shape[0]
    wide = 2 * HEAD_DIM
    sources = ((own, own_lane), (near, near_lane), (far, 0))
    mine, dq_lane = head * wide, 3 * wide + head * HEAD_DIM
    targets = ((grads, mine), (to_near, mine), (to_far, 0))
    both, raw, pairs, slopes = {}, {}, {}, {}
    over_channels = (((1,), (1,)), ((), ()))

    def rows(t):
        return pl.ds(t * BLOCK, BLOCK)

    def window(t):
        low, high = max(t - 1, 0), min(t + 1, time_blocks - 1)
        return low, high, pl.ds(low * BLOCK, (high - low + 1) * BLOCK)

    def products(t):
        q = qg[rows(t), qg_lane : qg_lane + HEAD_DIM]
        g = qg[rows(t), qg_lane + HEAD_DIM : qg_lane + wide]
        zero = jnp.zeros_like(q)
        both[t] = jnp.concatenate(
            [jnp.concatenate([q, zero], axis=1), jnp.concatenate([zero, g], axis=1)], axis=0
        )
        low, high, span = window(t)
        scores, probs = [], []
        top = None
        for block, (source, lane) in enumerate(sources):
            k = source[span, lane : lane + HEAD_DIM]
            v = source[span, lane + HEAD_DIM : lane + wide]
            s = lax.dot_general(k, q, over_channels, preferred_element_type=jnp.float32)
            probs.append(lax.dot_general(v, g, over_channels, preferred_element_type=jnp.float32))
            bias = [block_bias(bias_ref, t, near_t - t + 1, block) for near_t in range(low, high + 1)]
            s = s * SCALE + jnp.concatenate(bias, axis=0)
            block_top = jnp.max(s, axis=0, keepdims=True)
            top = block_top if top is None else jnp.maximum(top, block_top)
            scores.append(s)
        raw[t] = (scores, probs, top)

    def softmax(t):
        scores, probs, top = raw.pop(t)
        low, high, _ = window(t)
        total = jnp.zeros((1, BLOCK), jnp.float32)
        exps = []
        for s in scores:
            e = jnp.exp(s - top)
            total += jnp.sum(e, axis=0, keepdims=True)
            exps.append(e)
        inv = 1.0 / total
        row_dot = jnp.zeros((1, BLOCK), jnp.float32)
        attention = [e * inv for e in exps]
        for p, pg in zip(attention, probs):
            row_dot += jnp.sum(p.astype(jnp.bfloat16).astype(jnp.float32) * pg, axis=0, keepdims=True)
        return low, high, attention, probs, row_dot

    def slope(t, low, high, attention, probs, row_dot):
        slopes[t], pairs[t] = [], []
        for p, pg in zip(attention, probs):
            ds = (p * (pg - row_dot) * SCALE).astype(jnp.bfloat16)
            pair = jnp.concatenate([ds, p.astype(jnp.bfloat16)], axis=1)
            pairs[t].append([pair[i * BLOCK : (i + 1) * BLOCK] for i in range(high - low + 1)])
            slopes[t].append(ds)

    def to_query(t):
        _, _, span = window(t)
        keys = jnp.concatenate([source[span, lane : lane + HEAD_DIM] for source, lane in sources], axis=0)
        ds = jnp.concatenate(slopes.pop(t), axis=0)
        dq = lax.dot_general(ds, keys, (((0,), (0,)), ((), ())), preferred_element_type=jnp.float32)
        grads[rows(t), dq_lane : dq_lane + HEAD_DIM] = dq.astype(jnp.bfloat16)

    def to_keys(t):
        near_ts = [n for n in (t - 1, t, t + 1) if 0 <= n < time_blocks]
        w = jnp.concatenate([both[n] for n in near_ts], axis=0)
        x = [
            jnp.concatenate([pairs[n][block][t - max(n - 1, 0)] for n in near_ts], axis=1)
            for block in range(3)
        ]
        r = jnp.dot(jnp.concatenate(x, axis=0), w, preferred_element_type=jnp.float32)
        for block, (target, lane) in enumerate(targets):
            part = r[block * BLOCK : (block + 1) * BLOCK]
            target[rows(t), lane : lane + wide] = part.astype(jnp.bfloat16)

    products(0)
    for t in range(time_blocks):
        if t + 1 < time_blocks:
            products(t + 1)
        if t > 1:
            to_keys(t - 2)
        state = softmax(t)
        if t > 0:
            to_query(t - 1)
        slope(t, *state)
    to_query(time_blocks - 1)
    to_keys(time_blocks - 2)
    to_keys(time_blocks - 1)


def head_grads(bias, everything, near, far, shared, head, flops, after=()):
    rows = everything.shape[0]
    wide = 2 * HEAD_DIM
    lanes = ((HEADS_LOCAL + head) * wide, head * wide, head * wide, head)
    return pl.pallas_call(
        lambda *refs: grads_kernel(lanes, *refs),
        in_specs=[VMEM] * (5 + len(shared)) + [ANY] * len(after),
        out_specs=[VMEM] * 3,
        out_shape=[
            jax.ShapeDtypeStruct((rows, lanes_out), jnp.bfloat16)
            for lanes_out in (9 * HEAD_DIM, 6 * HEAD_DIM, wide)
        ],
        input_output_aliases={5 + i: i for i in range(len(shared))},
        compiler_params=pltpu.CompilerParams(vmem_limit_bytes=SMALL_LIMIT),
        cost_estimate=pl.CostEstimate(flops=flops, bytes_accessed=4_500_000, transcendentals=1_200_000),
        name="head_grads",
    )(bias, everything, everything, near, far, *shared, *after)


def add_halo(grads, halo, first, flops):
    lanes = slice(first * 2 * HEAD_DIM, first * 2 * HEAD_DIM + halo.shape[1])

    def kernel(grads, halo, out):
        total = grads[:, lanes].astype(jnp.float32) + halo[...].astype(jnp.float32)
        out[:, lanes] = total.astype(jnp.bfloat16)

    return pl.pallas_call(
        kernel,
        in_specs=[VMEM] * 2,
        out_specs=VMEM,
        out_shape=jax.ShapeDtypeStruct(grads.shape, grads.dtype),
        input_output_aliases={0: 0},
        compiler_params=pltpu.CompilerParams(vmem_limit_bytes=SMALL_LIMIT),
        cost_estimate=pl.CostEstimate(flops=flops, bytes_accessed=1000, transcendentals=0),
        name="add_halo",
    )(grads, halo)


def split_kernel(arrived, bias, near, *fars):
    wide = 2 * HEAD_DIM
    for j, far in enumerate(fars):
        far[...] = arrived[:, j * wide : (j + 1) * wide]
    near[...] = arrived[:, : HEADS_LOCAL * wide]


def split(arrived, bias):
    rows, wide = arrived.shape[0], 2 * HEAD_DIM
    far = jax.ShapeDtypeStruct((rows, wide), arrived.dtype)
    near = jax.ShapeDtypeStruct((rows, HEADS_LOCAL * wide), arrived.dtype)
    near, *fars = pl.pallas_call(
        split_kernel,
        in_specs=[VMEM, ANY],
        out_specs=[VMEM] * HEADS_LOCAL,
        out_shape=[near] + [far] * (HEADS_LOCAL - 1),
        compiler_params=pltpu.CompilerParams(vmem_limit_bytes=SMALL_LIMIT),
        cost_estimate=pl.CostEstimate(flops=0, bytes_accessed=1000, transcendentals=0),
        name="split",
    )(arrived, bias)
    return near, fars


def take_last(arrived, after):
    rows, wide = arrived.shape[0], 2 * HEAD_DIM

    def kernel(arrived, _, out):
        out[...] = arrived[:, (HEADS_LOCAL - 1) * wide : HEADS_LOCAL * wide]

    return pl.pallas_call(
        kernel,
        in_specs=[VMEM, ANY],
        out_specs=VMEM,
        out_shape=jax.ShapeDtypeStruct((rows, wide), arrived.dtype),
        compiler_params=pltpu.CompilerParams(vmem_limit_bytes=SMALL_LIMIT),
        cost_estimate=pl.CostEstimate(flops=0, bytes_accessed=1000, transcendentals=0),
        name="take_last",
    )(arrived, after)


def shards(queries, keys, values, out_grad, window_mask):
    swap, chain = swap_pairs(), chain_pairs()
    wide = 2 * HEAD_DIM
    everything = tuple((i, j) for j in range(HEADS_LOCAL) for i in (0, 1))
    everything += tuple((i, j) for j in range(HEADS_LOCAL) for i in (2, 3))
    packed = pack((keys, values, queries, out_grad), everything)
    packed, window_mask = lax.optimization_barrier((packed, window_mask))
    arrived = lax.all_to_all(packed, "ctx", 0, 0, tiled=True).reshape(1024, 12 * HEAD_DIM)
    bias = mask_bias(window_mask)
    for_near, for_far = split(arrived, bias)
    fars = [lax.ppermute(part, "ctx", chain) for part in for_far]
    near = lax.ppermute(for_near, "ctx", swap)
    fars.append(lax.ppermute(take_last(arrived, near), "ctx", chain))
    grads, to_near, to_far = head_grads(bias, arrived, near, fars[0], (), 0, 1_000_000_000)
    back = lax.ppermute(to_far, "ctx", chain)
    grads, to_near, to_far = head_grads(bias, arrived, near, fars[1], (grads, to_near), 1, 1_000_000_000)
    next_back = lax.ppermute(to_far, "ctx", chain)
    shared = (grads, to_near)
    grads, to_near, to_far = head_grads(bias, arrived, near, fars[2], shared, 2, 3_000_000_000)
    near_back = lax.ppermute(to_near, "ctx", swap)
    last_back = lax.ppermute(to_far, "ctx", chain)
    grads = add_halo(grads, back, 0, 3_000_000_000)
    grads = add_halo(grads, next_back, 1, 100_000_000_000)
    grads = add_halo(grads, near_back, 0, 1000)
    grads = add_halo(grads, last_back, 2, 1000)
    grads = lax.all_to_all(grads.reshape(32, 32, 9 * HEAD_DIM), "ctx", 0, 0, tiled=True)
    dk, dv, dq = unpack(grads)
    return dq, dk, dv


def solution(mesh):
    tokens = P("ctx", None, None, "head")
    return jax.shard_map(
        shards,
        mesh=mesh,
        in_specs=(tokens, tokens, tokens, tokens, P("ctx", None, None)),
        out_specs=(tokens, tokens, tokens),
        check_vma=False,
    )
```
